256 devices in a mesh: seq: 64 (over y, z, core), head: 4 (over x).
Axes of the slice: x: 4, y: 4, z: 8, core: 2. Of those that a mesh axis runs over, the one named last changes fastest.
Arguments:
- inputs: bfloat16 [32768, 1024], P('seq'), may hold values from -16 to 16
- proj_weight: bfloat16 [1024, 4096], P(None, 'head'), may hold values from -0.1875 to 0.1875
- out_weight: bfloat16 [1024, 1024], P(None, 'head'), may hold values from -0.1875 to 0.1875
- cotangent: bfloat16 [32768, 1024], P('seq'), may hold values from -16 to 16
- block_history: int32 [256], P('seq'), may hold values from 0 to 31, never falling along the last dimension, each value on 1 to 16 neighbouring positions
- event_mask: int32 [32768], P('seq'), may hold values 0 or 1
Outputs:
- layer_out: bfloat16 [32768, 1024], P('seq', 'head')
- grad_input: bfloat16 [32768, 1024], P('seq', 'head')
- grad_proj: float32 [1024, 4096], P('seq', 'head')
- grad_out: float32 [1024, 1024], P('seq', 'head')
The draws below stay inside these ranges and needn't reach their ends.
Inputs may be any that keep to these rules, and one draw needn't show every extreme that they name: `block_history`: ids never fall along the blocks; each history covers 1 to 16 consecutive blocks, and one covers exactly 16.
All inputs are finite; a program needn't handle non-finite values. No bound on the sum of `event_mask` on one device may be relied on, other than what follows from the above.
Results may differ from the reference program's by a relative error of at most 0.014.
Values may be sent and summed in bfloat16 or wider, within the bound.
A program may use at most 128 MiB of HBM per device.

```python
import math
import jax
import jax.numpy as jnp
import numpy as np
from jax import lax

D = 1024
HEADS = 8
DH = 128
BLK = 128
MAXB = 16
TOKENS = 32768
NBLOCKS = 256
HISTS = 32


def plant(entries, own_key, low, top_value):
    place = [jax.random.randint(jax.random.fold_in(own_key, axis), (), 0, length) for axis, length in enumerate(entries.shape)]
    main_axis = entries.shape.index(max(entries.shape))
    beside = place[:main_axis] + [(place[main_axis] + 1) % entries.shape[main_axis]] + place[main_axis + 1:]
    return entries.at[tuple(place)].set(low).at[tuple(beside)].set(top_value)


def raised(array, rng, source, target, parts, factor):
    def block_of(axis_at):
        return (jnp.arange(array.shape[axis_at]) // (array.shape[axis_at] // parts)).reshape((-1,) + (1,) * (array.ndim - 1 - axis_at))

    first = jax.random.permutation(rng, parts)[block_of(target)]
    far = (block_of(target) + parts // 2) % parts
    return jnp.where((block_of(source) == first) | (block_of(source) == far), factor * array, array)


def steps_of(stream_key, shape, shards, smallest, largest):
    level, own = 1.0, jax.random.fold_in(stream_key, 6)
    for position, parts in shards:
        heights = jnp.exp(jax.random.uniform(jax.random.fold_in(own, position), (parts,), jnp.float32, smallest / len(shards), largest / len(shards)))
        level = level * jnp.repeat(heights, shape[position] // parts).reshape([-1 if axis == position else 1 for axis in range(len(shape))])
    return level


def split_up(amount, total, limit, skew):
    loads = [(1 << 20) // math.isqrt(standing ** skew) + 1 for standing in range(2, amount + 1)]
    rest, holding = total - limit - (amount - 1), [1] * (amount - 1)
    while rest > 0:
        movable = [i for i in range(amount - 1) if holding[i] < limit]
        mass, left = sum([loads[i] for i in movable]), rest
        for i in movable:
            addition = min(limit - holding[i], max(1, left * loads[i] // mass), rest)
            holding[i] = holding[i] + addition
            rest = rest - addition
    return np.array([limit] + holding)


def ragged(rng, number_of, total, reach, lean):
    if number_of == 2:
        one = jax.random.randint(rng, (), max(1, total - reach), min(reach, total - 1) + 1)
        return jnp.stack([one, total - one])
    lengths = jnp.asarray(split_up(number_of, total, reach, lean), jnp.int32)
    pairs = (number_of - 1) // 2
    source_of, taker = lengths[1:1 + 2 * pairs:2], lengths[2:2 + 2 * pairs:2]
    room = jnp.minimum(source_of - 1, reach - taker)
    shifted = jax.random.randint(jax.random.fold_in(rng, 1), (pairs,), 0, 1 << 20) % (room + 1)
    lengths = lengths.at[1:1 + 2 * pairs:2].set(source_of - shifted).at[2:2 + 2 * pairs:2].set(taker + shifted)
    return lengths[jax.random.permutation(jax.random.fold_in(rng, 2), number_of)]


def bell_draw(own_key, shape, deviation, limit, shards=(), held_as=jnp.bfloat16):
    loudness = steps_of(own_key, shape, shards, -0.22, 0.18) if shards else 1.0
    drawn = jax.random.normal(own_key, shape, jnp.float32) * deviation * loudness
    return jnp.minimum(jnp.maximum(drawn, -limit), limit).astype(held_as)


def heavy_noise(rng, extent, deviation, limit, shards, heavy, kind=jnp.bfloat16):
    result = deviation * jax.random.normal(rng, extent, jnp.float32)
    if shards:
        result = result * steps_of(rng, extent, shards, -0.22, 0.18)
    return jnp.clip(raised(result, jax.random.fold_in(rng, 3), *heavy), -limit, limit).astype(kind)


def setup_inputs(seed: int = 0) -> dict:
    splits = jax.random.split(jax.random.key(seed), 7)
    return {
        "inputs": heavy_noise(splits[0], (TOKENS, D), 1.0, 16.0, ((0, 64),), (0, 1, 64, 4.0)),
        "proj_weight": bell_draw(splits[1], (D, 4 * D), D ** -0.5, 0.1875, ((1, 4),)),
        "out_weight": bell_draw(splits[2], (D, D), D ** -0.5, 0.1875, ((1, 4),)),
        "cotangent": heavy_noise(splits[3], (TOKENS, D), 1.0, 16.0, ((0, 64),), (0, 1, 64, 4.0)),
        "block_history": jnp.searchsorted(jnp.cumsum(ragged(splits[4], HISTS, NBLOCKS, MAXB, 2)), jnp.arange(NBLOCKS), side="right").astype(jnp.int32),
        "event_mask": plant((jax.random.randint(splits[5], (TOKENS,), 0, 8) < 7).astype(jnp.int32), jax.random.fold_in(splits[5], 1), 0, 1),
    }


def silu_slope(values_in):
    logistic = jax.nn.sigmoid(values_in)
    return logistic * (1.0 + values_in * (1.0 - logistic))

def round_bf16(values_in):
    return lax.optimization_barrier(values_in.astype(jnp.bfloat16)).astype(jnp.float32)

def reference(inputs, proj_weight, out_weight, cotangent, block_history, event_mask):
    token_count = inputs.shape[0]
    block_count = block_history.shape[0]
    score_scale = DH ** (-0.5)
    margin = (MAXB - 1) * BLK
    window_len = margin + BLK
    projected = jnp.dot(inputs, proj_weight, preferred_element_type=jnp.float32)
    activated = round_bf16(jax.nn.silu(projected)).reshape(token_count, HEADS, 4, DH)
    gate_rows = activated[:, :, 0]
    value_rows = activated[:, :, 1]
    query_rows = activated[:, :, 2]
    key_rows = activated[:, :, 3]
    history_ids = jnp.repeat(block_history, BLK)
    front_zeros = jnp.zeros((margin, HEADS, DH), jnp.float32)
    padded_keys = jnp.concatenate([front_zeros, key_rows], axis=0)
    padded_values = jnp.concatenate([front_zeros, value_rows], axis=0)
    padded_ids = jnp.concatenate([jnp.full((margin,), -1, jnp.int32), history_ids.astype(jnp.int32)])
    padded_mask = jnp.concatenate([jnp.zeros((margin,), jnp.int32), event_mask.astype(jnp.int32)])
    key_offsets = lax.iota(jnp.int32, window_len) - margin
    query_offsets = lax.iota(jnp.int32, BLK)

    def block_view(block_index):
        first_row = (block_index * BLK).astype(jnp.int32)
        queries = lax.dynamic_slice_in_dim(query_rows, first_row, BLK, 0)
        key_block = lax.dynamic_slice_in_dim(padded_keys, first_row, window_len, 0)
        value_block = lax.dynamic_slice_in_dim(padded_values, first_row, window_len, 0)
        query_ids = lax.dynamic_slice_in_dim(history_ids, first_row, BLK, 0)
        query_mask = lax.dynamic_slice_in_dim(event_mask, first_row, BLK, 0)
        key_ids = lax.dynamic_slice_in_dim(padded_ids, first_row, window_len, 0)
        key_mask = lax.dynamic_slice_in_dim(padded_mask, first_row, window_len, 0)
        allowed = ((query_ids[:, None] == key_ids[None, :]) & (query_mask[:, None] > 0) & (key_mask[None, :] > 0) & (key_offsets[None, :] <= query_offsets[:, None])).astype(jnp.float32)
        scores = jnp.einsum('thd,shd->hts', queries, key_block) * score_scale
        return (first_row, queries, key_block, value_block, allowed, scores)

    def block_forward(block_index):
        first_row, queries, key_block, value_block, allowed, scores = block_view(block_index)
        weights = round_bf16(allowed[None] * jax.nn.silu(scores))
        return jnp.einsum('hts,shd->thd', weights, value_block)
    block_ids = jnp.arange(block_count, dtype=jnp.int32)
    attention = lax.map(block_forward, block_ids).reshape(token_count, D)
    row_mean = lax.optimization_barrier(jnp.sum(attention, axis=1, keepdims=True)) / D
    row_square = lax.optimization_barrier(jnp.sum(attention * attention, axis=1, keepdims=True)) / D
    inverse_std = lax.rsqrt(row_square - row_mean * row_mean + 1e-05)
    normed = (attention - row_mean) * inverse_std
    gate_flat = gate_rows.reshape(token_count, D)
    mixed = (normed * gate_flat).astype(jnp.bfloat16)
    layer_out = (inputs.astype(jnp.float32) + jnp.dot(mixed, out_weight.T, preferred_element_type=jnp.float32)).astype(jnp.bfloat16)
    grad_mixed = jnp.dot(cotangent, out_weight, preferred_element_type=jnp.float32)
    grad_normed = grad_mixed * gate_flat
    grad_gate = grad_mixed * normed
    mean_grad = lax.optimization_barrier(jnp.sum(grad_normed, axis=1, keepdims=True)) / D
    mean_cross = lax.optimization_barrier(jnp.sum(grad_normed * normed, axis=1, keepdims=True)) / D
    grad_attention = round_bf16((grad_normed - mean_grad - normed * mean_cross) * inverse_std).reshape(token_count, HEADS, DH)

    def block_grad(carry, block_index):
        key_total, value_total = carry
        first_row, queries, key_block, value_block, allowed, scores = block_view(block_index)
        grad_block = lax.dynamic_slice_in_dim(grad_attention, first_row, BLK, 0)
        weights = round_bf16(allowed[None] * jax.nn.silu(scores))
        grad_weights = jnp.einsum('thd,shd->hts', grad_block, value_block)
        grad_scores = round_bf16(allowed[None] * grad_weights * silu_slope(scores))
        grad_query = jnp.einsum('hts,shd->thd', grad_scores, key_block) * score_scale
        grad_key = jnp.einsum('hts,thd->shd', grad_scores, queries) * score_scale
        grad_value = jnp.einsum('hts,thd->shd', weights, grad_block)
        key_total = lax.dynamic_update_slice_in_dim(key_total, lax.dynamic_slice_in_dim(key_total, first_row, window_len, 0) + grad_key, first_row, 0)
        value_total = lax.dynamic_update_slice_in_dim(value_total, lax.dynamic_slice_in_dim(value_total, first_row, window_len, 0) + grad_value, first_row, 0)
        return ((key_total, value_total), grad_query)
    zero_total = jnp.zeros((margin + token_count, HEADS, DH), jnp.float32)
    (key_total, value_total), grad_queries = lax.scan(block_grad, (zero_total, zero_total), block_ids)
    grad_query = grad_queries.reshape(token_count, HEADS, DH)
    grad_key = key_total[margin:]
    grad_value = value_total[margin:]
    grad_act = jnp.stack([grad_gate.reshape(token_count, HEADS, DH), grad_value, grad_query, grad_key], axis=2)
    grad_pre = (grad_act.reshape(token_count, 4 * D) * silu_slope(projected)).astype(jnp.bfloat16)
    grad_scale = token_count ** (-0.5)
    grad_proj = jnp.dot(inputs.T, grad_pre, preferred_element_type=jnp.float32) * grad_scale
    grad_out = jnp.dot(cotangent.T, mixed, preferred_element_type=jnp.float32) * grad_scale
    grad_input = (cotangent.astype(jnp.float32) + jnp.dot(grad_pre, proj_weight.T, preferred_element_type=jnp.float32)).astype(jnp.bfloat16)
    return (layer_out, grad_input, grad_proj, grad_out)
```

```python
import functools

import jax
import jax.numpy as jnp
from jax import lax
from jax.experimental import pallas as pl
from jax.experimental.pallas import tpu as pltpu
from jax.sharding import PartitionSpec as P

MESH = pl.DeviceIdType.MESH
DH = 128
BLK = 128
TILE = 256
F32 = jnp.float32
BF16 = jnp.bfloat16
NT = (((1,), (1,)), ((), ()))
MAX_COPIES = 96


def dot_nt(a, b):
    return lax.dot_general(a, b, NT, preferred_element_type=F32)


def dot_nn(a, b):
    return jnp.dot(a, b, preferred_element_type=F32)


def silu_parts(u, mask):
    t = jnp.tanh(u)
    p = 1.0 + t
    if mask is not None:
        p = p * mask
    w = u * p
    return w, p + w * (1.0 - t)


def layer_kernel(
    nx,
    ny,
    nz,
    token_total,
    inp,
    wp_hbm,
    wo_hbm,
    cot,
    history,
    events,
    lo_ref,
    gi_ref,
    gp_ref,
    go_ref,
    wp,
    wo,
    wpp,
    xs,
    cs,
    xt,
    ct,
    metas,
    ids,
    mk,
    mcol,
    slope,
    gate,
    kv,
    qh,
    dah,
    attn,
    gm,
    stat,
    mx,
    m2,
    gpre,
    g2,
    dq,
    dk,
    dv,
    lo_bufs,
    gi_bufs,
    w_bufs,
    w_s2,
    w_r2,
    fin,
    fin_r,
    lsem,
    ssem,
    rsem,
):
    s = lax.axis_index("seq")
    x = lax.axis_index("head")
    r = lax.rem(s, 2)
    o = 1 - r
    c = s // 2
    nc = ny * nz
    z = lax.rem(c, nz)
    y = c // nz
    half = inp.shape[0]
    T = 2 * half
    D = inp.shape[1]
    CW = D // nx
    RY = D // ny
    RZ = RY // nz
    RC = RZ // 2
    nblk = T // BLK
    ntile = T // TILE
    scale = DH ** (-0.5)
    grad_scale = token_total ** (-0.5)

    own0 = pl.multiple_of(r * half, half)
    oth0 = pl.multiple_of(o * half, half)
    own_rows = pl.ds(own0, half)
    oth_rows = pl.ds(oth0, half)
    head_cols = pl.ds(pl.multiple_of(r * 4 * DH, 4 * DH), 4 * DH)
    head_dh = pl.ds(pl.multiple_of(r * DH, DH), DH)
    oth_dh = pl.ds(pl.multiple_of(o * DH, DH), DH)

    load_x = pltpu.make_async_copy(inp, xs.at[own_rows], lsem.at[0])
    load_wp = pltpu.make_async_copy(wp_hbm, wp, lsem.at[1])
    load_c = pltpu.make_async_copy(cot, cs.at[own_rows], lsem.at[2])
    load_wo = pltpu.make_async_copy(wo_hbm, wo, lsem.at[3])
    for copy in (load_x, load_wp, load_c, load_wo):
        copy.start()

    def at_chip(chip):
        return (chip * 2 + r, x)

    chip_next = [lax.rem(c + d, nc) for d in (1, 2)]
    chip_prev = [lax.rem(c + nc - d, nc) for d in (1, 2)]
    partner = (c * 2 + o, x)

    def at_x(dx):
        return (s, lax.rem(x + nx + dx, nx))

    def at_y(dy):
        return at_chip(lax.rem(y + ny + dy, ny) * nz + z)

    def at_z(dz):
        return at_chip(y * nz + lax.rem(z + dz, nz))

    group = []
    for dx in range(nx):
        for dr in range(2):
            if dx or dr:
                group.append((c * 2 + lax.rem(r + dr, 2), lax.rem(x + dx, nx)))
    peers = list(group)
    peers += [at_chip(k) for k in chip_next + chip_prev]
    peers += [at_y(d) for d in ((1, -1) if ny > 2 else (1,))]
    peers += [at_z(d) for d in range(1, nz)]

    barrier = pltpu.get_barrier_semaphore()
    for peer in peers:
        pl.semaphore_signal(barrier, inc=1, device_id=peer, device_id_type=MESH)

    sent = []

    def push(src, dst, device):
        i = len(sent)
        copy = pltpu.make_async_remote_copy(
            src_ref=src,
            dst_ref=dst,
            send_sem=ssem.at[i],
            recv_sem=rsem.at[i],
            device_id=device,
            device_id_type=MESH,
        )
        copy.start()
        sent.append(copy)
        return copy

    def mask_columns(block_meta, row0):
        for b in range(nblk // 2):
            row = block_meta[4 + b : 5 + b, :].astype(F32)
            mcol[pl.ds(row0 + b * BLK, BLK), :] = jnp.broadcast_to(row, (BLK, BLK)).T

    def project(row0):
        def step(t, carry):
            rows = pl.ds(pl.multiple_of(row0 + t * TILE, TILE), TILE)
            act, slope2 = silu_parts(dot_nn(xs[rows, :], wp[:, head_cols]) * 0.5, None)
            slope[rows, :] = 0.5 * slope2
            m = mcol[rows, :]
            gate[rows, :] = act[:, :DH].astype(BF16)
            kv[0, rows, DH:] = act[:, DH : 2 * DH].astype(BF16)
            qh[0, rows, :] = (act[:, 2 * DH : 3 * DH] * m).astype(BF16)
            kv[0, rows, :DH] = (act[:, 3 * DH :] * m).astype(BF16)
            return carry

        lax.fori_loop(0, half // TILE, step, 0)

    own_meta = jnp.concatenate(
        [jnp.full((1, BLK), history[b], jnp.int32) for b in range(nblk // 2)] + [events[...]],
        axis=0,
    )
    metas[r] = own_meta
    mask_columns(own_meta, own0)
    load_x.wait()
    load_wp.wait()
    project(own0)

    pl.semaphore_wait(barrier, len(peers))
    swap_x = push(inp, xs.at[own_rows], partner)
    swap_meta = push(metas.at[r], metas.at[r], partner)
    kv_a = push(kv.at[0, own_rows], kv.at[1, own_rows], at_chip(chip_next[0]))
    q_a = push(qh.at[0, own_rows], qh.at[1, own_rows], at_chip(chip_prev[0]))
    swap_c = push(cot, cs.at[own_rows], partner)

    swap_meta.wait_recv()
    mask_columns(metas[o], oth0)
    swap_x.wait_recv()
    project(oth0)
    kv_b = push(kv.at[0, oth_rows], kv.at[1, oth_rows], at_chip(chip_next[0]))
    q_b = push(qh.at[0, oth_rows], qh.at[1, oth_rows], at_chip(chip_prev[0]))

    ids[0] = jnp.concatenate([metas[0][:4], metas[1][:4]], axis=0)
    id_copies = [
        push(ids.at[0], ids.at[1], at_chip(chip_next[0])),
        push(ids.at[0], ids.at[2], at_chip(chip_next[1])),
        push(ids.at[0], ids.at[3], at_chip(chip_prev[0])),
        push(ids.at[0], ids.at[4], at_chip(chip_prev[1])),
    ]

    def block_masks(slot):
        own = ids[0]
        other = ids[slot]
        for k in range(nblk):
            same = jnp.broadcast_to(other[k : k + 1, :], own.shape) == own
            mk[slot, :, k * BLK : (k + 1) * BLK] = jnp.where(same, 1.0, 0.0)

    def tile_rows(t):
        return pl.ds(t * TILE if isinstance(t, int) else pl.multiple_of(t * TILE, TILE), TILE)

    def tile_mask(slot, t, first, last):
        cols = slice(first * TILE, last * TILE)
        n = (last - first) * TILE
        return jnp.concatenate(
            [
                jnp.broadcast_to(mk[slot, pl.ds((TILE // BLK) * t + i, 1), cols], (BLK, n))
                for i in range(TILE // BLK)
            ],
            axis=0,
        )

    def triangle(lower):
        row = lax.broadcasted_iota(jnp.int32, (TILE, TILE), 0)
        col = lax.broadcasted_iota(jnp.int32, (TILE, TILE), 1)
        return jnp.where(col <= row if lower else row <= col, 1.0, 0.0)

    def query_mask(slot, t, first, last):
        mask = tile_mask(slot, t, first, last)
        if slot == 0:
            n = mask.shape[1] - TILE
            corner = mask[:, n:] * triangle(True)
            mask = jnp.concatenate([mask[:, :n], corner], axis=1) if n else corner
        return mask

    def key_mask(slot, t, first, last):
        mask = tile_mask(slot, t, first, last)
        if slot == 0:
            n = mask.shape[1] - TILE
            corner = mask[:, :TILE] * triangle(False)
            mask = jnp.concatenate([corner, mask[:, TILE:]], axis=1) if n else corner
        return mask

    def put(ref, rows, part, begin):
        ref[rows, :] = part if begin else ref[rows, :] + part

    def over_tiles(step, spans):
        if spans is None:
            def body(t, carry):
                step(t, 0, ntile)
                return carry

            lax.fori_loop(0, ntile, body, 0)
        else:
            for t in range(ntile):
                step(t, *spans(t))

    def upto(t):
        return 0, t + 1

    def onward(t):
        return t, ntile

    def attend(slot, spans):
        def step(t, first, last):
            rows = tile_rows(t)
            cols = slice(first * TILE, last * TILE)
            u = dot_nt(qh[0, rows, :], kv[slot, cols, :DH]) * (0.5 * scale)
            w = u * (1.0 + jnp.tanh(u)) * query_mask(slot, t, first, last)
            put(attn, rows, dot_nn(w.astype(BF16), kv[slot, cols, DH:]), slot == 0)

        over_tiles(step, spans)

    block_masks(0)
    attend(0, upto)

    load_wo.wait()
    load_c.wait()
    swap_c.wait_recv()

    def grad_mix(t, carry):
        rows = tile_rows(t)
        gm[rows, :] = dot_nn(cs[rows, :], wo[:, head_dh])
        return carry

    lax.fori_loop(0, ntile, grad_mix, 0)

    kv_a.wait_recv()
    kv_fa = push(kv.at[1, own_rows], kv.at[2, own_rows], at_chip(chip_next[0]))
    q_a.wait_recv()
    q_fa = push(qh.at[1, own_rows], qh.at[2, own_rows], at_chip(chip_prev[0]))

    def turn(b, carry):
        rows = pl.ds(pl.multiple_of(b * BLK, BLK), BLK)
        xt[:, rows] = xs[rows, :].T
        ct[:, rows] = cs[rows, :].T
        return carry

    lax.fori_loop(0, nblk // 2, turn, 0)

    kv_b.wait_recv()
    kv_fb = push(kv.at[1, oth_rows], kv.at[2, oth_rows], at_chip(chip_next[0]))
    q_b.wait_recv()
    q_fb = push(qh.at[1, oth_rows], qh.at[2, oth_rows], at_chip(chip_prev[0]))
    for copy in id_copies:
        copy.wait_recv()
    for slot in range(1, 5):
        block_masks(slot)
    attend(1, None)
    lax.fori_loop(nblk // 2, nblk, turn, 0)
    for h in range(2):
        for i, p in enumerate((0, 2, 1, 3)):
            wpp[:, (4 * h + i) * DH : (4 * h + i + 1) * DH] = wp[
                :, (4 * h + p) * DH : (4 * h + p + 1) * DH
            ]
    kv_fa.wait_recv()
    kv_fb.wait_recv()
    attend(2, onward)

    lane = lax.broadcasted_iota(jnp.int32, (BLK, BLK), 1)
    for b in range(nblk // 2):
        packed = []
        for h in range(2):
            rows = pl.ds(h * half + b * BLK, BLK)
            a = attn[rows, :]
            gn = gm[rows, :] * gate[rows, :].astype(F32)
            sums = [a, a * a, gn, gn * a]
            column = jnp.zeros((BLK, BLK), F32)
            for i, term in enumerate(sums):
                total = jnp.sum(term, axis=1, keepdims=True)
                column = jnp.where(lane == 4 * h + i, total, column)
            packed.append(column)
        stat[0, :, b * BLK : (b + 1) * BLK] = (packed[0] + packed[1]).T[:8, :]
    stat_copies = [
        push(stat.at[0], stat.at[i + 1], device) for i, device in enumerate(group)
    ]
    for copy in stat_copies:
        copy.wait_recv()
    total = stat[0]
    for i in range(len(group)):
        total = total + stat[i + 1]
    derived = []
    for h in range(2):
        s1, s2, s3, s4 = [total[4 * h + i : 4 * h + i + 1, :] for i in range(4)]
        mean = s1 / D
        inv = lax.rsqrt(s2 / D - mean * mean + 1e-05)
        derived += [mean, inv, s3 / D, (s4 - mean * s3) * inv / D]
    derived = jnp.concatenate(derived, axis=0)

    da_copies = []
    for h in range(2):
        for b in range(nblk // 2):
            rows = pl.ds(h * half + b * BLK, BLK)
            columns = jnp.concatenate(
                [derived[:, b * BLK : (b + 1) * BLK], jnp.zeros((BLK - 8, BLK), F32)], axis=0
            ).T
            mean, inv, mean_grad, mean_cross = [
                columns[:, 4 * h + i : 4 * h + i + 1] for i in range(4)
            ]
            g = gate[rows, :].astype(F32)
            grad_mixed = gm[rows, :]
            normed = (attn[rows, :] - mean) * inv
            mx[rows, :] = (normed * g).astype(BF16)
            dah[0, rows, :] = (
                (grad_mixed * g - mean_grad - normed * mean_cross) * inv
            ).astype(BF16)
            gpre[rows, :DH] = (grad_mixed * normed * slope[rows, :DH]).astype(BF16)
        rows = pl.ds(h * half, half)
        da_copies.append(
            push(dah.at[0, rows], dah.at[1, rows], at_chip(chip_prev[0]))
        )

    swap_mx = push(mx.at[oth_rows], m2.at[:, head_dh], partner)
    m2[:, head_dh] = mx[own_rows, :]

    def query_grads(slot, spans):
        def step(t, first, last):
            rows = tile_rows(t)
            cols = slice(first * TILE, last * TILE)
            u = dot_nt(qh[0, rows, :], kv[slot, cols, :DH]) * (0.5 * scale)
            gw = dot_nt(dah[0, rows, :], kv[slot, cols, DH:])
            w, slope2 = silu_parts(u, query_mask(slot, t, first, last))
            put(dq, rows, dot_nn((gw * slope2).astype(BF16), kv[slot, cols, :DH]), slot == 0)

        over_tiles(step, spans)

    def key_grads(j, spans):
        slot = 0 if j == 0 else 2 + j

        def step(t, first, last):
            rows = tile_rows(t)
            cols = slice(first * TILE, last * TILE)
            u = dot_nt(kv[0, rows, :DH], qh[j, cols, :]) * (0.5 * scale)
            gw = dot_nt(kv[0, rows, DH:], dah[j, cols, :])
            w, slope2 = silu_parts(u, key_mask(slot, t, first, last))
            put(dv, rows, dot_nn(w.astype(BF16), dah[j, cols, :]), j == 0)
            put(dk, rows, dot_nn((gw * slope2).astype(BF16), qh[j, cols, :]), j == 0)

        over_tiles(step, spans)

    def ring_first(n, device, term, bufs, cols):
        send, far, near, last, own = bufs
        h = far.shape[0] // 2
        copies = []
        if n == 4:
            send[0, :, cols] = term(2).astype(BF16)
            copies = [
                push(send.at[0, :h, cols], far.at[:h, cols], device(1)),
                push(send.at[0, h:, cols], far.at[h:, cols], device(-1)),
            ]
        near[0, :, cols] = term(1)
        if n == 4:
            near[1, :, cols] = term(3)
        own[:, cols] = term(0)
        return copies

    def ring_second(n, device, bufs, cols, copies):
        send, far, near, last, own = bufs
        h = far.shape[0] // 2
        out = []
        if n == 4:
            copies[0].wait_recv()
            send[1, :h, cols] = (near[0, :h, cols] + far[:h, cols].astype(F32)).astype(BF16)
            send[1, h:, cols] = near[0, h:, cols].astype(BF16)
        else:
            send[1, :, cols] = near[0, :, cols].astype(BF16)
        out.append(push(send.at[1, :, cols], last.at[0, :, cols], device(1)))
        if n == 4:
            copies[1].wait_recv()
            send[2, :h, cols] = near[1, :h, cols].astype(BF16)
            send[2, h:, cols] = (near[1, h:, cols] + far[h:, cols].astype(F32)).astype(BF16)
            out.append(push(send.at[2, :, cols], last.at[1, :, cols], device(-1)))
        return out

    def ring_total(bufs, cols, copies):
        send, far, near, last, own = bufs
        for copy in copies:
            copy.wait_recv()
        part = own[:, cols]
        for i in range(len(copies)):
            part = part + last[i, :, cols].astype(F32)
        return part

    def weight_term(lhs_t, rhs):
        def term(d):
            at = pl.multiple_of(lax.rem(y + d, ny) * RY, RY)
            return dot_nn(lhs_t[pl.ds(at, RY), :], rhs)

        return term

    def model_term(rows_ref, weight):
        def term(d):
            at = pl.multiple_of(lax.rem(x + d, nx) * CW, CW)
            return dot_nt(rows_ref[...], weight[pl.ds(at, CW), :])

        return term

    def over_z(cols, copies):
        part = ring_total(w_bufs, cols, copies)
        w_bufs[4][:, cols] = part
        w_s2[:, cols] = part.astype(BF16)
        later = []
        for dz in range(1, nz):
            at = pl.multiple_of(lax.rem(z + dz, nz) * RZ, RZ)
            later.append(
                push(w_s2.at[pl.ds(at, RZ), cols], w_r2.at[dz - 1, :, cols], at_z(dz))
            )
        return later

    every = pl.ds(0, CW)
    out_cols, gate_cols, query_cols = [pl.ds(i * DH, DH) for i in range(3)]
    early_cols, late_cols = pl.ds(0, 3 * DH), pl.ds(3 * DH, 2 * DH)

    query_grads(0, upto)
    swap_mx.wait_recv()
    lo_first = ring_first(nx, at_x, model_term(m2, wo), lo_bufs, every)
    da_copies[0].wait_recv()
    rows = pl.ds(0, half)
    da_fa = push(dah.at[1, rows], dah.at[2, rows], at_chip(chip_prev[0]))
    query_grads(1, None)
    da_copies[1].wait_recv()
    rows = pl.ds(half, half)
    da_fb = push(dah.at[1, rows], dah.at[2, rows], at_chip(chip_prev[0]))
    lo_second = ring_second(nx, at_x, lo_bufs, every, lo_first)
    out_first = ring_first(ny, at_y, weight_term(ct, mx[...]), w_bufs, out_cols)
    gate_first = ring_first(ny, at_y, weight_term(xt, gpre[:, :DH]), w_bufs, gate_cols)
    query_grads(2, onward)
    gpre[:, DH : 2 * DH] = (
        dq[...] * mcol[...] * (0.5 * scale) * slope[:, 2 * DH : 3 * DH]
    ).astype(BF16)
    early = pl.ds(pl.multiple_of(r * 4 * DH, 4 * DH), 2 * DH)
    late = pl.ds(pl.multiple_of(r * 4 * DH + 2 * DH, 2 * DH), 2 * DH)
    swap_early = push(gpre.at[oth_rows, : 2 * DH], g2.at[:, early], partner)
    query_first = ring_first(ny, at_y, weight_term(xt, gpre[:, DH : 2 * DH]), w_bufs, query_cols)
    out_second = ring_second(ny, at_y, w_bufs, out_cols, out_first)
    gate_second = ring_second(ny, at_y, w_bufs, gate_cols, gate_first)
    key_grads(0, onward)
    query_second = ring_second(ny, at_y, w_bufs, query_cols, query_first)
    q_fa.wait_recv()
    q_fb.wait_recv()
    key_grads(1, None)
    parts = [
        ring_total(w_bufs, cols, copies)
        for cols, copies in (
            (out_cols, out_second),
            (gate_cols, gate_second),
            (query_cols, query_second),
        )
    ]
    w_bufs[4][:, early_cols] = jnp.concatenate(parts, axis=1)
    early_z = over_z(early_cols, [])
    da_fa.wait_recv()
    da_fb.wait_recv()
    key_grads(2, upto)
    gpre[:, 2 * DH : 3 * DH] = (dv[...] * slope[:, DH : 2 * DH]).astype(BF16)
    gpre[:, 3 * DH :] = (dk[...] * mcol[...] * (0.5 * scale) * slope[:, 3 * DH :]).astype(BF16)
    swap_late = push(gpre.at[oth_rows, 2 * DH :], g2.at[:, late], partner)
    g2[:, head_cols] = gpre[own_rows, :]
    late_first = ring_first(ny, at_y, weight_term(xt, gpre[:, 2 * DH :]), w_bufs, late_cols)
    swap_early.wait_recv()
    swap_late.wait_recv()
    gi_first = ring_first(nx, at_x, model_term(g2, wpp), gi_bufs, every)
    late_second = ring_second(ny, at_y, w_bufs, late_cols, late_first)
    gi_second = ring_second(nx, at_x, gi_bufs, every, gi_first)
    late_z = over_z(late_cols, late_second)

    model_cols = pl.ds(pl.multiple_of(x * CW, CW), CW)
    lo = ring_total(lo_bufs, every, lo_second)
    lo_ref[...] = (xs[own_rows, model_cols].astype(F32) + lo).astype(BF16)

    for copy in early_z + late_z:
        copy.wait_recv()
    part = w_bufs[4][pl.ds(pl.multiple_of(z * RZ, RZ), RZ), :]
    for i in range(nz - 1):
        part = part + w_r2[i].astype(F32)
    fin[...] = part * grad_scale
    oth_part = pl.ds(pl.multiple_of(o * RC, RC), RC)
    own_part = pl.ds(pl.multiple_of(r * RC, RC), RC)
    swap_w = push(fin.at[oth_part], fin_r, partner)

    gi = ring_total(gi_bufs, every, gi_second)
    gi_ref[...] = (cs[own_rows, model_cols].astype(F32) + gi).astype(BF16)

    swap_w.wait_recv()
    for side, src, rows in ((r, fin, own_part), (o, fin_r, pl.ds(0, RC))):
        go_ref[:, pl.ds(pl.multiple_of(side * DH, DH), DH)] = src[rows, :DH]
        for p, i in enumerate((1, 3, 2, 4)):
            cols = pl.ds(pl.multiple_of(side * 4 * DH + p * DH, DH), DH)
            gp_ref[:, cols] = src[rows, i * DH : (i + 1) * DH]

    for copy in sent:
        copy.wait_send()


def hand_on(*refs):
    n = len(refs) // 2
    for src, dst in zip(refs[:n], refs[n:]):
        dst[...] = src[...]


def body(nx, ny, nz, inputs, proj_weight, out_weight, cotangent, block_history, event_mask):
    half, D = inputs.shape
    T = 2 * half
    CW = D // nx
    RY = D // ny
    RZ = RY // nz
    nblk = half // BLK
    vmem = pl.BlockSpec(memory_space=pltpu.VMEM)
    hbm = pl.BlockSpec(memory_space=pltpu.HBM)
    V = pltpu.VMEM

    def ring_bufs(rows, cols):
        return (
            V((3, rows, cols), BF16),
            V((rows, cols), BF16),
            V((2, rows, cols), F32),
            V((2, rows, cols), BF16),
            V((rows, cols), F32),
        )

    out_shape = (
        jax.ShapeDtypeStruct((half, CW), BF16),
        jax.ShapeDtypeStruct((half, CW), BF16),
        jax.ShapeDtypeStruct((RZ // 2, 8 * DH), F32),
        jax.ShapeDtypeStruct((RZ // 2, 2 * DH), F32),
    )
    results = pl.pallas_call(
        functools.partial(layer_kernel, nx, ny, nz, half * 2 * ny * nz),
        out_shape=out_shape,
        in_specs=[hbm] * 4 + [pl.BlockSpec(memory_space=pltpu.SMEM), vmem],
        out_specs=(vmem,) * 4,
        scratch_shapes=[
            V((D, 8 * DH), BF16),
            V((D, 2 * DH), BF16),
            V((D, 8 * DH), BF16),
            V((T, D), BF16),
            V((T, D), BF16),
            V((D, T), BF16),
            V((D, T), BF16),
            V((2, 8, BLK), jnp.int32),
            V((5, 8, BLK), jnp.int32),
            V((5, 8, T), F32),
            V((T, DH), F32),
            V((T, 4 * DH), F32),
            V((T, DH), BF16),
            V((3, T, 2 * DH), BF16),
            V((3, T, DH), BF16),
            V((3, T, DH), BF16),
            V((T, DH), F32),
            V((T, DH), F32),
            V((2 * nx, 8, half), F32),
            V((T, DH), BF16),
            V((half, 2 * DH), BF16),
            V((T, 4 * DH), BF16),
            V((half, 8 * DH), BF16),
            V((T, DH), F32),
            V((T, DH), F32),
            V((T, DH), F32),
            ring_bufs(half, CW),
            ring_bufs(half, CW),
            ring_bufs(RY, 5 * DH),
            V((RY, 5 * DH), BF16),
            V((nz - 1, RZ, 5 * DH), BF16),
            V((RZ, 5 * DH), F32),
            V((RZ // 2, 5 * DH), F32),
            pltpu.SemaphoreType.DMA((4,)),
            pltpu.SemaphoreType.DMA((MAX_COPIES,)),
            pltpu.SemaphoreType.DMA((MAX_COPIES,)),
        ],
        compiler_params=pltpu.CompilerParams(
            collective_id=0, has_side_effects=True, vmem_limit_bytes=56 * 1024 * 1024
        ),
    )(
        inputs,
        proj_weight,
        out_weight,
        cotangent,
        block_history,
        event_mask.reshape(nblk, BLK),
    )
    return pl.pallas_call(
        hand_on, out_shape=out_shape, in_specs=[vmem] * 4, out_specs=(vmem,) * 4
    )(*results)


def solution(mesh):
    nx = mesh.shape["head"]
    chips = mesh.shape["seq"] // 2
    nz = 8 if chips % 32 == 0 else 2
    ny = chips // nz
    return jax.shard_map(
        functools.partial(body, nx, ny, nz),
        mesh=mesh,
        in_specs=(
            P("seq", None),
            P(None, "head"),
            P(None, "head"),
            P("seq", None),
            P("seq"),
            P("seq"),
        ),
        out_specs=(P("seq", "head"), P("seq", "head"), P("seq", "head"), P("seq", "head")),
        check_vma=False,
    )
```

```python
import functools

import jax
import jax.numpy as jnp
from jax import lax
from jax.experimental import pallas as pl
from jax.experimental.pallas import tpu as pltpu
from jax.sharding import PartitionSpec as P

MESH = pl.DeviceIdType.MESH
DH = 128
BLK = 128
TILE = 256
F32 = jnp.float32
BF16 = jnp.bfloat16
NT = (((1,), (1,)), ((), ()))
MAX_COPIES = 96


def dot_nt(a, b):
    return lax.dot_general(a, b, NT, preferred_element_type=F32)


def dot_nn(a, b):
    return jnp.dot(a, b, preferred_element_type=F32)


def silu_parts(u, mask):
    t = jnp.tanh(u)
    p = 1.0 + t
    if mask is not None:
        p = p * mask
    w = u * p
    return w, p + w * (1.0 - t)


def layer_kernel(
    nx,
    ny,
    nz,
    token_total,
    inp,
    wp_hbm,
    wo_hbm,
    cot,
    history,
    events,
    lo_ref,
    gi_ref,
    gp_ref,
    go_ref,
    wp,
    wo,
    wpp,
    xs,
    cs,
    xt,
    ct,
    metas,
    ids,
    mk,
    mcol,
    slope,
    gate,
    kv,
    qh,
    dah,
    attn,
    gm,
    stat,
    mx,
    m2,
    gpre,
    g2,
    dq,
    dk,
    dv,
    lo_bufs,
    gi_bufs,
    w_bufs,
    w_s2,
    w_r2,
    fin,
    fin_r,
    q_slopes,
    k_weights,
    k_slopes,
    lsem,
    ssem,
    rsem,
):
    s = lax.axis_index("seq")
    x = lax.axis_index("head")
    r = lax.rem(s, 2)
    o = 1 - r
    c = s // 2
    nc = ny * nz
    z = lax.rem(c, nz)
    y = c // nz
    half = inp.shape[0]
    T = 2 * half
    D = inp.shape[1]
    CW = D // nx
    RY = D // ny
    RZ = RY // nz
    RC = RZ // 2
    nblk = T // BLK
    ntile = T // TILE
    scale = DH ** (-0.5)
    grad_scale = token_total ** (-0.5)

    own0 = pl.multiple_of(r * half, half)
    oth0 = pl.multiple_of(o * half, half)
    own_rows = pl.ds(own0, half)
    oth_rows = pl.ds(oth0, half)
    head_cols = pl.ds(pl.multiple_of(r * 4 * DH, 4 * DH), 4 * DH)
    head_dh = pl.ds(pl.multiple_of(r * DH, DH), DH)
    oth_dh = pl.ds(pl.multiple_of(o * DH, DH), DH)

    load_x = pltpu.make_async_copy(inp, xs.at[own_rows], lsem.at[0])
    load_wp = pltpu.make_async_copy(wp_hbm, wp, lsem.at[1])
    load_c = pltpu.make_async_copy(cot, cs.at[own_rows], lsem.at[2])
    load_wo = pltpu.make_async_copy(wo_hbm, wo, lsem.at[3])
    for copy in (load_x, load_wp, load_c, load_wo):
        copy.start()

    def at_chip(chip):
        return (chip * 2 + r, x)

    chip_next = [lax.rem(c + d, nc) for d in (1, 2)]
    chip_prev = [lax.rem(c + nc - d, nc) for d in (1, 2)]
    partner = (c * 2 + o, x)

    def at_x(dx):
        return (s, lax.rem(x + nx + dx, nx))

    def at_y(dy):
        return at_chip(lax.rem(y + ny + dy, ny) * nz + z)

    def at_z(dz):
        return at_chip(y * nz + lax.rem(z + dz, nz))

    group = []
    for dx in range(nx):
        for dr in range(2):
            if dx or dr:
                group.append((c * 2 + lax.rem(r + dr, 2), lax.rem(x + dx, nx)))
    peers = list(group)
    peers += [at_chip(k) for k in chip_next + chip_prev]
    peers += [at_y(d) for d in ((1, -1) if ny > 2 else (1,))]
    peers += [at_z(d) for d in range(1, nz)]

    barrier = pltpu.get_barrier_semaphore()
    for peer in peers:
        pl.semaphore_signal(barrier, inc=1, device_id=peer, device_id_type=MESH)

    sent = []

    def push(src, dst, device):
        i = len(sent)
        copy = pltpu.make_async_remote_copy(
            src_ref=src,
            dst_ref=dst,
            send_sem=ssem.at[i],
            recv_sem=rsem.at[i],
            device_id=device,
            device_id_type=MESH,
        )
        copy.start()
        sent.append(copy)
        return copy

    def mask_columns(block_meta, row0):
        for b in range(nblk // 2):
            row = block_meta[4 + b : 5 + b, :].astype(F32)
            mcol[pl.ds(row0 + b * BLK, BLK), :] = jnp.broadcast_to(row, (BLK, BLK)).T

    def project(row0):
        def step(t, carry):
            rows = pl.ds(pl.multiple_of(row0 + t * TILE, TILE), TILE)
            act, slope2 = silu_parts(dot_nn(xs[rows, :], wp[:, head_cols]) * 0.5, None)
            slope[rows, :] = 0.5 * slope2
            m = mcol[rows, :]
            gate[rows, :] = act[:, :DH].astype(BF16)
            kv[0, rows, DH:] = act[:, DH : 2 * DH].astype(BF16)
            qh[0, rows, :] = (act[:, 2 * DH : 3 * DH] * m).astype(BF16)
            kv[0, rows, :DH] = (act[:, 3 * DH :] * m).astype(BF16)
            return carry

        lax.fori_loop(0, half // TILE, step, 0)

    own_meta = jnp.concatenate(
        [jnp.full((1, BLK), history[b], jnp.int32) for b in range(nblk // 2)] + [events[...]],
        axis=0,
    )
    metas[r] = own_meta
    mask_columns(own_meta, own0)
    load_x.wait()
    load_wp.wait()
    project(own0)

    pl.semaphore_wait(barrier, len(peers))
    swap_x = push(inp, xs.at[own_rows], partner)
    swap_meta = push(metas.at[r], metas.at[r], partner)
    kv_a = push(kv.at[0, own_rows], kv.at[1, own_rows], at_chip(chip_next[0]))
    q_a = push(qh.at[0, own_rows], qh.at[1, own_rows], at_chip(chip_prev[0]))
    swap_c = push(cot, cs.at[own_rows], partner)

    swap_meta.wait_recv()
    mask_columns(metas[o], oth0)
    swap_x.wait_recv()
    project(oth0)
    kv_b = push(kv.at[0, oth_rows], kv.at[1, oth_rows], at_chip(chip_next[0]))
    q_b = push(qh.at[0, oth_rows], qh.at[1, oth_rows], at_chip(chip_prev[0]))

    ids[0] = jnp.concatenate([metas[0][:4], metas[1][:4]], axis=0)
    id_copies = [
        push(ids.at[0], ids.at[1], at_chip(chip_next[0])),
        push(ids.at[0], ids.at[2], at_chip(chip_next[1])),
        push(ids.at[0], ids.at[3], at_chip(chip_prev[0])),
        push(ids.at[0], ids.at[4], at_chip(chip_prev[1])),
    ]

    def block_masks(slot):
        own = ids[0]
        other = ids[slot]
        for k in range(nblk):
            same = jnp.broadcast_to(other[k : k + 1, :], own.shape) == own
            mk[slot, :, k * BLK : (k + 1) * BLK] = jnp.where(same, 1.0, 0.0)

    def tile_rows(t):
        return pl.ds(t * TILE if isinstance(t, int) else pl.multiple_of(t * TILE, TILE), TILE)

    def tile_mask(slot, t, first, last):
        cols = slice(first * TILE, last * TILE)
        n = (last - first) * TILE
        return jnp.concatenate(
            [
                jnp.broadcast_to(mk[slot, pl.ds((TILE // BLK) * t + i, 1), cols], (BLK, n))
                for i in range(TILE // BLK)
            ],
            axis=0,
        )

    def triangle(lower):
        row = lax.broadcasted_iota(jnp.int32, (TILE, TILE), 0)
        col = lax.broadcasted_iota(jnp.int32, (TILE, TILE), 1)
        return jnp.where(col <= row if lower else row <= col, 1.0, 0.0)

    def query_mask(slot, t, first, last):
        mask = tile_mask(slot, t, first, last)
        if slot == 0:
            n = mask.shape[1] - TILE
            corner = mask[:, n:] * triangle(True)
            mask = jnp.concatenate([mask[:, :n], corner], axis=1) if n else corner
        return mask

    def key_mask(slot, t, first, last):
        mask = tile_mask(slot, t, first, last)
        if slot == 0:
            n = mask.shape[1] - TILE
            corner = mask[:, :TILE] * triangle(False)
            mask = jnp.concatenate([corner, mask[:, TILE:]], axis=1) if n else corner
        return mask

    def put(ref, rows, part, begin):
        ref[rows, :] = part if begin else ref[rows, :] + part

    def over_tiles(step, spans):
        if spans is None:
            def body(t, carry):
                step(t, 0, ntile)
                return carry

            lax.fori_loop(0, ntile, body, 0)
        else:
            for t in range(ntile):
                step(t, *spans(t))

    def upto(t):
        return 0, t + 1

    def onward(t):
        return t, ntile

    def kept(bufs, j, shifted, rows, first, last):
        shift = 1 if j == shifted else 0
        cols = slice((first + shift) * TILE, (last + shift) * TILE)
        return bufs[j % 2].at[rows, cols]

    def attend(slot, spans, sums=True, slopes=True):
        def step(t, first, last):
            rows = tile_rows(t)
            cols = slice(first * TILE, last * TILE)
            u = dot_nt(qh[0, rows, :], kv[slot, cols, :DH]) * (0.5 * scale)
            w, slope2 = silu_parts(u, query_mask(slot, t, first, last))
            if sums:
                put(attn, rows, dot_nn(w.astype(BF16), kv[slot, cols, DH:]), slot == 0)
            if slopes:
                kept(q_slopes, slot, 2, rows, first, last)[...] = slope2.astype(BF16)

        over_tiles(step, spans)

    def key_parts(j, spans):
        slot = 0 if j == 0 else 2 + j

        def step(t, first, last):
            rows = tile_rows(t)
            cols = slice(first * TILE, last * TILE)
            u = dot_nt(kv[0, rows, :DH], qh[j, cols, :]) * (0.5 * scale)
            w, slope2 = silu_parts(u, key_mask(slot, t, first, last))
            kept(k_weights, j, 0, rows, first, last)[...] = w.astype(BF16)
            kept(k_slopes, j, 0, rows, first, last)[...] = slope2.astype(BF16)

        over_tiles(step, spans)

    block_masks(0)
    attend(0, upto)

    load_wo.wait()
    load_c.wait()
    swap_c.wait_recv()

    def grad_mix(t, carry):
        rows = tile_rows(t)
        gm[rows, :] = dot_nn(cs[rows, :], wo[:, head_dh])
        return carry

    lax.fori_loop(0, ntile, grad_mix, 0)

    kv_a.wait_recv()
    kv_fa = push(kv.at[1, own_rows], kv.at[2, own_rows], at_chip(chip_next[0]))
    q_a.wait_recv()
    q_fa = push(qh.at[1, own_rows], qh.at[2, own_rows], at_chip(chip_prev[0]))

    def turn(b, carry):
        rows = pl.ds(pl.multiple_of(b * BLK, BLK), BLK)
        xt[:, rows] = xs[rows, :].T
        ct[:, rows] = cs[rows, :].T
        return carry

    key_parts(0, onward)

    kv_b.wait_recv()
    kv_fb = push(kv.at[1, oth_rows], kv.at[2, oth_rows], at_chip(chip_next[0]))
    q_b.wait_recv()
    q_fb = push(qh.at[1, oth_rows], qh.at[2, oth_rows], at_chip(chip_prev[0]))
    for copy in id_copies:
        copy.wait_recv()
    for slot in range(1, 5):
        block_masks(slot)
    attend(1, None)
    key_parts(1, None)
    lax.fori_loop(0, nblk, turn, 0)
    for h in range(2):
        for i, p in enumerate((0, 2, 1, 3)):
            wpp[:, (4 * h + i) * DH : (4 * h + i + 1) * DH] = wp[
                :, (4 * h + p) * DH : (4 * h + p + 1) * DH
            ]
    q_fa.wait_recv()
    q_fb.wait_recv()
    key_parts(2, upto)
    kv_fa.wait_recv()
    kv_fb.wait_recv()
    attend(2, onward, slopes=False)

    lane = lax.broadcasted_iota(jnp.int32, (BLK, BLK), 1)
    for b in range(nblk // 2):
        packed = []
        for h in range(2):
            rows = pl.ds(h * half + b * BLK, BLK)
            a = attn[rows, :]
            gn = gm[rows, :] * gate[rows, :].astype(F32)
            sums = [a, a * a, gn, gn * a]
            column = jnp.zeros((BLK, BLK), F32)
            for i, term in enumerate(sums):
                total = jnp.sum(term, axis=1, keepdims=True)
                column = jnp.where(lane == 4 * h + i, total, column)
            packed.append(column)
        stat[0, :, b * BLK : (b + 1) * BLK] = (packed[0] + packed[1]).T[:8, :]
    stat_copies = [
        push(stat.at[0], stat.at[i + 1], device) for i, device in enumerate(group)
    ]
    attend(2, onward, sums=False)
    for copy in stat_copies:
        copy.wait_recv()
    total = stat[0]
    for i in range(len(group)):
        total = total + stat[i + 1]
    derived = []
    for h in range(2):
        s1, s2, s3, s4 = [total[4 * h + i : 4 * h + i + 1, :] for i in range(4)]
        mean = s1 / D
        inv = lax.rsqrt(s2 / D - mean * mean + 1e-05)
        derived += [mean, inv, s3 / D, (s4 - mean * s3) * inv / D]
    derived = jnp.concatenate(derived, axis=0)

    da_copies = []
    for h in range(2):
        for b in range(nblk // 2):
            rows = pl.ds(h * half + b * BLK, BLK)
            columns = jnp.concatenate(
                [derived[:, b * BLK : (b + 1) * BLK], jnp.zeros((BLK - 8, BLK), F32)], axis=0
            ).T
            mean, inv, mean_grad, mean_cross = [
                columns[:, 4 * h + i : 4 * h + i + 1] for i in range(4)
            ]
            g = gate[rows, :].astype(F32)
            grad_mixed = gm[rows, :]
            normed = (attn[rows, :] - mean) * inv
            mx[rows, :] = (normed * g).astype(BF16)
            dah[0, rows, :] = (
                (grad_mixed * g - mean_grad - normed * mean_cross) * inv
            ).astype(BF16)
            gpre[rows, :DH] = (grad_mixed * normed * slope[rows, :DH]).astype(BF16)
        rows = pl.ds(h * half, half)
        da_copies.append(
            push(dah.at[0, rows], dah.at[1, rows], at_chip(chip_prev[0]))
        )

    swap_mx = push(mx.at[oth_rows], m2.at[:, head_dh], partner)
    m2[:, head_dh] = mx[own_rows, :]

    def query_grads(slot, spans):
        def step(t, first, last):
            rows = tile_rows(t)
            cols = slice(first * TILE, last * TILE)
            gw = dot_nt(dah[0, rows, :], kv[slot, cols, DH:]).astype(BF16)
            ds = gw * kept(q_slopes, slot, 2, rows, first, last)[...]
            put(dq, rows, dot_nn(ds, kv[slot, cols, :DH]), slot == 0)

        over_tiles(step, spans)

    def key_grads(j, spans):
        def step(t, first, last):
            rows = tile_rows(t)
            cols = slice(first * TILE, last * TILE)
            gw = dot_nt(kv[0, rows, DH:], dah[j, cols, :]).astype(BF16)
            ds = gw * kept(k_slopes, j, 0, rows, first, last)[...]
            w = kept(k_weights, j, 0, rows, first, last)[...]
            put(dv, rows, dot_nn(w, dah[j, cols, :]), j == 0)
            put(dk, rows, dot_nn(ds, qh[j, cols, :]), j == 0)

        over_tiles(step, spans)

    def ring_first(n, device, term, bufs, cols):
        send, far, near, last, own = bufs
        h = far.shape[0] // 2
        copies = []
        if n == 4:
            send[0, :, cols] = term(2).astype(BF16)
            copies = [
                push(send.at[0, :h, cols], far.at[:h, cols], device(1)),
                push(send.at[0, h:, cols], far.at[h:, cols], device(-1)),
            ]
        near[0, :, cols] = term(1)
        if n == 4:
            near[1, :, cols] = term(3)
        own[:, cols] = term(0)
        return copies

    def ring_second(n, device, bufs, cols, copies):
        send, far, near, last, own = bufs
        h = far.shape[0] // 2
        out = []
        if n == 4:
            copies[0].wait_recv()
            send[1, :h, cols] = (near[0, :h, cols] + far[:h, cols].astype(F32)).astype(BF16)
            send[1, h:, cols] = near[0, h:, cols].astype(BF16)
        else:
            send[1, :, cols] = near[0, :, cols].astype(BF16)
        out.append(push(send.at[1, :, cols], last.at[0, :, cols], device(1)))
        if n == 4:
            copies[1].wait_recv()
            send[2, :h, cols] = near[1, :h, cols].astype(BF16)
            send[2, h:, cols] = (near[1, h:, cols] + far[h:, cols].astype(F32)).astype(BF16)
            out.append(push(send.at[2, :, cols], last.at[1, :, cols], device(-1)))
        return out

    def ring_total(bufs, cols, copies):
        send, far, near, last, own = bufs
        for copy in copies:
            copy.wait_recv()
        part = own[:, cols]
        for i in range(len(copies)):
            part = part + last[i, :, cols].astype(F32)
        return part

    def weight_term(lhs_t, rhs):
        def term(d):
            at = pl.multiple_of(lax.rem(y + d, ny) * RY, RY)
            return dot_nn(lhs_t[pl.ds(at, RY), :], rhs)

        return term

    def model_term(rows_ref, weight):
        def term(d):
            at = pl.multiple_of(lax.rem(x + d, nx) * CW, CW)
            return dot_nt(rows_ref[...], weight[pl.ds(at, CW), :])

        return term

    def over_z(cols, copies):
        part = ring_total(w_bufs, cols, copies)
        w_bufs[4][:, cols] = part
        w_s2[:, cols] = part.astype(BF16)
        later = []
        for dz in range(1, nz):
            at = pl.multiple_of(lax.rem(z + dz, nz) * RZ, RZ)
            later.append(
                push(w_s2.at[pl.ds(at, RZ), cols], w_r2.at[dz - 1, :, cols], at_z(dz))
            )
        return later

    every = pl.ds(0, CW)
    out_cols, gate_cols, query_cols = [pl.ds(i * DH, DH) for i in range(3)]
    early_cols, late_cols = pl.ds(0, 3 * DH), pl.ds(3 * DH, 2 * DH)

    query_grads(0, upto)
    swap_mx.wait_recv()
    lo_first = ring_first(nx, at_x, model_term(m2, wo), lo_bufs, every)
    da_copies[0].wait_recv()
    rows = pl.ds(0, half)
    da_fa = push(dah.at[1, rows], dah.at[2, rows], at_chip(chip_prev[0]))
    query_grads(1, None)
    da_copies[1].wait_recv()
    rows = pl.ds(half, half)
    da_fb = push(dah.at[1, rows], dah.at[2, rows], at_chip(chip_prev[0]))
    lo_second = ring_second(nx, at_x, lo_bufs, every, lo_first)
    out_first = ring_first(ny, at_y, weight_term(ct, mx[...]), w_bufs, out_cols)
    gate_first = ring_first(ny, at_y, weight_term(xt, gpre[:, :DH]), w_bufs, gate_cols)
    query_grads(2, onward)
    gpre[:, DH : 2 * DH] = (
        dq[...] * mcol[...] * (0.5 * scale) * slope[:, 2 * DH : 3 * DH]
    ).astype(BF16)
    early = pl.ds(pl.multiple_of(r * 4 * DH, 4 * DH), 2 * DH)
    late = pl.ds(pl.multiple_of(r * 4 * DH + 2 * DH, 2 * DH), 2 * DH)
    swap_early = push(gpre.at[oth_rows, : 2 * DH], g2.at[:, early], partner)
    query_first = ring_first(ny, at_y, weight_term(xt, gpre[:, DH : 2 * DH]), w_bufs, query_cols)
    out_second = ring_second(ny, at_y, w_bufs, out_cols, out_first)
    gate_second = ring_second(ny, at_y, w_bufs, gate_cols, gate_first)
    key_grads(0, onward)
    query_second = ring_second(ny, at_y, w_bufs, query_cols, query_first)
    key_grads(1, None)
    parts = [
        ring_total(w_bufs, cols, copies)
        for cols, copies in (
            (out_cols, out_second),
            (gate_cols, gate_second),
            (query_cols, query_second),
        )
    ]
    w_bufs[4][:, early_cols] = jnp.concatenate(parts, axis=1)
    early_z = over_z(early_cols, [])
    da_fa.wait_recv()
    da_fb.wait_recv()
    key_grads(2, upto)
    gpre[:, 2 * DH : 3 * DH] = (dv[...] * slope[:, DH : 2 * DH]).astype(BF16)
    gpre[:, 3 * DH :] = (dk[...] * mcol[...] * (0.5 * scale) * slope[:, 3 * DH :]).astype(BF16)
    swap_late = push(gpre.at[oth_rows, 2 * DH :], g2.at[:, late], partner)
    g2[:, head_cols] = gpre[own_rows, :]
    late_first = ring_first(ny, at_y, weight_term(xt, gpre[:, 2 * DH :]), w_bufs, late_cols)
    swap_early.wait_recv()
    swap_late.wait_recv()
    gi_first = ring_first(nx, at_x, model_term(g2, wpp), gi_bufs, every)
    late_second = ring_second(ny, at_y, w_bufs, late_cols, late_first)
    gi_second = ring_second(nx, at_x, gi_bufs, every, gi_first)
    late_z = over_z(late_cols, late_second)

    model_cols = pl.ds(pl.multiple_of(x * CW, CW), CW)
    lo = ring_total(lo_bufs, every, lo_second)
    lo_ref[...] = (xs[own_rows, model_cols].astype(F32) + lo).astype(BF16)

    for copy in early_z + late_z:
        copy.wait_recv()
    part = w_bufs[4][pl.ds(pl.multiple_of(z * RZ, RZ), RZ), :]
    for i in range(nz - 1):
        part = part + w_r2[i].astype(F32)
    fin[...] = part * grad_scale
    oth_part = pl.ds(pl.multiple_of(o * RC, RC), RC)
    own_part = pl.ds(pl.multiple_of(r * RC, RC), RC)
    swap_w = push(fin.at[oth_part], fin_r, partner)

    gi = ring_total(gi_bufs, every, gi_second)
    gi_ref[...] = (cs[own_rows, model_cols].astype(F32) + gi).astype(BF16)

    swap_w.wait_recv()
    for side, src, rows in ((r, fin, own_part), (o, fin_r, pl.ds(0, RC))):
        go_ref[:, pl.ds(pl.multiple_of(side * DH, DH), DH)] = src[rows, :DH]
        for p, i in enumerate((1, 3, 2, 4)):
            cols = pl.ds(pl.multiple_of(side * 4 * DH + p * DH, DH), DH)
            gp_ref[:, cols] = src[rows, i * DH : (i + 1) * DH]

    for copy in sent:
        copy.wait_send()


def hand_on(*refs):
    n = len(refs) // 2
    copies = [
        pltpu.make_async_copy(refs[i], refs[n + i], refs[2 * n].at[i]) for i in range(n)
    ]
    for copy in copies:
        copy.start()
    for copy in copies:
        copy.wait()


def body(nx, ny, nz, inputs, proj_weight, out_weight, cotangent, block_history, event_mask):
    half, D = inputs.shape
    T = 2 * half
    CW = D // nx
    RY = D // ny
    RZ = RY // nz
    nblk = half // BLK
    vmem = pl.BlockSpec(memory_space=pltpu.VMEM)
    hbm = pl.BlockSpec(memory_space=pltpu.HBM)
    V = pltpu.VMEM

    def ring_bufs(rows, cols):
        return (
            V((3, rows, cols), BF16),
            V((rows, cols), BF16),
            V((2, rows, cols), F32),
            V((2, rows, cols), BF16),
            V((rows, cols), F32),
        )

    def pair_bufs():
        return V((T, T + TILE), BF16), V((T, T), BF16)

    out_shape = (
        jax.ShapeDtypeStruct((half, CW), BF16),
        jax.ShapeDtypeStruct((half, CW), BF16),
        jax.ShapeDtypeStruct((RZ // 2, 8 * DH), F32),
        jax.ShapeDtypeStruct((RZ // 2, 2 * DH), F32),
    )
    results = pl.pallas_call(
        functools.partial(layer_kernel, nx, ny, nz, half * 2 * ny * nz),
        out_shape=out_shape,
        in_specs=[hbm] * 4 + [pl.BlockSpec(memory_space=pltpu.SMEM), vmem],
        out_specs=(vmem,) * 4,
        scratch_shapes=[
            V((D, 8 * DH), BF16),
            V((D, 2 * DH), BF16),
            V((D, 8 * DH), BF16),
            V((T, D), BF16),
            V((T, D), BF16),
            V((D, T), BF16),
            V((D, T), BF16),
            V((2, 8, BLK), jnp.int32),
            V((5, 8, BLK), jnp.int32),
            V((5, 8, T), F32),
            V((T, DH), F32),
            V((T, 4 * DH), F32),
            V((T, DH), BF16),
            V((3, T, 2 * DH), BF16),
            V((3, T, DH), BF16),
            V((3, T, DH), BF16),
            V((T, DH), F32),
            V((T, DH), F32),
            V((2 * nx, 8, half), F32),
            V((T, DH), BF16),
            V((half, 2 * DH), BF16),
            V((T, 4 * DH), BF16),
            V((half, 8 * DH), BF16),
            V((T, DH), F32),
            V((T, DH), F32),
            V((T, DH), F32),
            ring_bufs(half, CW),
            ring_bufs(half, CW),
            ring_bufs(RY, 5 * DH),
            V((RY, 5 * DH), BF16),
            V((nz - 1, RZ, 5 * DH), BF16),
            V((RZ, 5 * DH), F32),
            V((RZ // 2, 5 * DH), F32),
            pair_bufs(),
            pair_bufs(),
            pair_bufs(),
            pltpu.SemaphoreType.DMA((4,)),
            pltpu.SemaphoreType.DMA((MAX_COPIES,)),
            pltpu.SemaphoreType.DMA((MAX_COPIES,)),
        ],
        compiler_params=pltpu.CompilerParams(
            collective_id=0, has_side_effects=True, vmem_limit_bytes=60 * 1024 * 1024
        ),
    )(
        inputs,
        proj_weight,
        out_weight,
        cotangent,
        block_history,
        event_mask.reshape(nblk, BLK),
    )
    return pl.pallas_call(
        hand_on,
        out_shape=out_shape,
        in_specs=[hbm] * 4,
        out_specs=(hbm,) * 4,
        scratch_shapes=[pltpu.SemaphoreType.DMA((4,))],
        compiler_params=pltpu.CompilerParams(vmem_limit_bytes=60 * 1024 * 1024),
    )(*results)


def solution(mesh):
    nx = mesh.shape["head"]
    chips = mesh.shape["seq"] // 2
    nz = 8 if chips % 32 == 0 else 2
    ny = chips // nz
    return jax.shard_map(
        functools.partial(body, nx, ny, nz),
        mesh=mesh,
        in_specs=(
            P("seq", None),
            P(None, "head"),
            P(None, "head"),
            P("seq", None),
            P("seq"),
            P("seq"),
        ),
        out_specs=(P("seq", "head"), P("seq", "head"), P("seq", "head"), P("seq", "head")),
        check_vma=False,
    )
```

```python
import functools

import jax
import jax.numpy as jnp
from jax import lax
from jax.experimental import pallas as pl
from jax.experimental.pallas import tpu as pltpu
from jax.sharding import PartitionSpec as P

MESH = pl.DeviceIdType.MESH
DH = 128
BLK = 128
TILE = 256
F32 = jnp.float32
BF16 = jnp.bfloat16
NT = (((1,), (1,)), ((), ()))
MAX_COPIES = 128


def dot_nt(a, b):
    return lax.dot_general(a, b, NT, preferred_element_type=F32)


def dot_nn(a, b):
    return jnp.dot(a, b, preferred_element_type=F32)


def silu_parts(u, mask):
    t = jnp.tanh(u)
    p = 1.0 + t
    if mask is not None:
        p = p * mask
    w = u * p
    return w, p + w * (1.0 - t)


def layer_kernel(
    nx,
    ny,
    nz,
    token_total,
    inp,
    wp_hbm,
    wo_hbm,
    cot,
    history,
    events,
    lo_ref,
    gi_ref,
    gp_ref,
    go_ref,
    wp,
    wo,
    wpp,
    xs,
    cs,
    xt,
    ct,
    metas,
    ids,
    mk,
    mcol,
    slope,
    gate,
    kv,
    qh,
    dah,
    attn,
    gm,
    stat,
    mx,
    m2,
    gpre,
    g2,
    dq,
    dk,
    dv,
    lo_bufs,
    gi_bufs,
    w_bufs,
    w_s2,
    w_r2,
    q_slopes,
    k_weights,
    k_slopes,
    lsem,
    ssem,
    rsem,
):
    s = lax.axis_index("seq")
    x = lax.axis_index("head")
    r = lax.rem(s, 2)
    o = 1 - r
    c = s // 2
    nc = ny * nz
    z = lax.rem(c, nz)
    y = c // nz
    half = inp.shape[0]
    T = 2 * half
    D = inp.shape[1]
    CW = D // nx
    RY = D // ny
    RZ = RY // nz
    RC = RZ // 2
    nblk = T // BLK
    ntile = T // TILE
    scale = DH ** (-0.5)
    grad_scale = token_total ** (-0.5)

    own0 = pl.multiple_of(r * half, half)
    oth0 = pl.multiple_of(o * half, half)
    own_rows = pl.ds(own0, half)
    oth_rows = pl.ds(oth0, half)
    head_cols = pl.ds(pl.multiple_of(r * 4 * DH, 4 * DH), 4 * DH)
    head_dh = pl.ds(pl.multiple_of(r * DH, DH), DH)

    load_x = pltpu.make_async_copy(inp, xs.at[own_rows], lsem.at[0])
    load_wp = pltpu.make_async_copy(wp_hbm, wp, lsem.at[1])
    load_c = pltpu.make_async_copy(cot, cs.at[own_rows], lsem.at[2])
    load_wo = pltpu.make_async_copy(wo_hbm, wo, lsem.at[3])
    for copy in (load_x, load_wp, load_c, load_wo):
        copy.start()

    def at_chip(chip):
        return (chip * 2 + r, x)

    chip_next = [lax.rem(c + d, nc) for d in (1, 2)]
    chip_prev = [lax.rem(c + nc - d, nc) for d in (1, 2)]
    partner = (c * 2 + o, x)

    def at_x(dx):
        return (s, lax.rem(x + nx + dx, nx))

    def at_y(dy):
        return at_chip(lax.rem(y + ny + dy, ny) * nz + z)

    def at_z(dz, dr):
        chip = y * nz + lax.rem(z + dz, nz)
        return (chip * 2 + lax.rem(r + dr, 2), x)

    group = []
    for dx in range(nx):
        for dr in range(2):
            if dx or dr:
                group.append((c * 2 + lax.rem(r + dr, 2), lax.rem(x + dx, nx)))
    peers = list(group)
    peers += [at_chip(k) for k in chip_next + chip_prev]
    peers += [at_y(d) for d in ((1, -1) if ny > 2 else (1,))]
    peers += [at_z(d, e) for d in range(1, nz) for e in range(2)]

    barrier = pltpu.get_barrier_semaphore()
    for peer in peers:
        pl.semaphore_signal(barrier, inc=1, device_id=peer, device_id_type=MESH)

    sent = []

    def push(src, dst, device):
        i = len(sent)
        copy = pltpu.make_async_remote_copy(
            src_ref=src,
            dst_ref=dst,
            send_sem=ssem.at[i],
            recv_sem=rsem.at[i],
            device_id=device,
            device_id_type=MESH,
        )
        copy.start()
        sent.append(copy)
        return copy

    def mask_columns(block_meta, row0):
        for b in range(nblk // 2):
            row = block_meta[4 + b : 5 + b, :].astype(F32)
            mcol[pl.ds(row0 + b * BLK, BLK), :] = jnp.broadcast_to(row, (BLK, BLK)).T

    def project(row0):
        def step(t, carry):
            rows = pl.ds(pl.multiple_of(row0 + t * TILE, TILE), TILE)
            p = dot_nn(xs[rows, :], wp[:, head_cols]) * 0.5
            slope[rows, :] = p
            u = p[:, DH:]
            act = u * (1.0 + jnp.tanh(u))
            m = mcol[rows, :]
            kv[0, rows, DH:] = act[:, :DH].astype(BF16)
            qh[0, rows, :] = (act[:, DH : 2 * DH] * m).astype(BF16)
            kv[0, rows, :DH] = (act[:, 2 * DH :] * m).astype(BF16)
            return carry

        lax.fori_loop(0, half // TILE, step, 0)

    def gates_and_slopes(t, carry):
        rows = pl.ds(pl.multiple_of(t * BLK, BLK), BLK)
        act, slope2 = silu_parts(slope[rows, :], None)
        gate[rows, :] = act[:, :DH].astype(BF16)
        slope[rows, :] = 0.5 * slope2
        return carry

    own_meta = jnp.concatenate(
        [jnp.full((1, BLK), history[b], jnp.int32) for b in range(nblk // 2)] + [events[...]],
        axis=0,
    )
    metas[r] = own_meta
    mask_columns(own_meta, own0)
    load_x.wait()
    load_wp.wait()
    project(own0)

    pl.semaphore_wait(barrier, len(peers))
    swap_x = push(xs.at[own_rows], xs.at[own_rows], partner)
    swap_meta = push(metas.at[r], metas.at[r], partner)
    kv_a = push(kv.at[0, own_rows], kv.at[1, own_rows], at_chip(chip_next[0]))
    q_a = push(qh.at[0, own_rows], qh.at[1, own_rows], at_chip(chip_prev[0]))
    load_c.wait()
    swap_c = push(cs.at[own_rows], cs.at[own_rows], partner)

    swap_meta.wait_recv()
    mask_columns(metas[o], oth0)
    swap_x.wait_recv()
    project(oth0)
    kv_b = push(kv.at[0, oth_rows], kv.at[1, oth_rows], at_chip(chip_next[0]))
    q_b = push(qh.at[0, oth_rows], qh.at[1, oth_rows], at_chip(chip_prev[0]))

    ids[0] = jnp.concatenate([metas[0][:4], metas[1][:4]], axis=0)
    id_copies = [
        push(ids.at[0], ids.at[1], at_chip(chip_next[0])),
        push(ids.at[0], ids.at[2], at_chip(chip_next[1])),
        push(ids.at[0], ids.at[3], at_chip(chip_prev[0])),
        push(ids.at[0], ids.at[4], at_chip(chip_prev[1])),
    ]

    def block_masks(slot):
        own = ids[0]
        other = ids[slot]
        for k in range(nblk):
            same = jnp.broadcast_to(other[k : k + 1, :], own.shape) == own
            mk[slot, :, k * BLK : (k + 1) * BLK] = jnp.where(same, 1.0, 0.0)

    def tile_rows(t):
        return pl.ds(t * TILE if isinstance(t, int) else pl.multiple_of(t * TILE, TILE), TILE)

    def tile_mask(slot, t, first, last):
        cols = slice(first * TILE, last * TILE)
        n = (last - first) * TILE
        return jnp.concatenate(
            [
                jnp.broadcast_to(
                    mk[slot, pl.ds((TILE // BLK) * t + i, 1), cols].astype(BF16), (BLK, n)
                )
                for i in range(TILE // BLK)
            ],
            axis=0,
        )

    def triangle(lower):
        row = lax.broadcasted_iota(jnp.int32, (TILE, TILE), 0)
        col = lax.broadcasted_iota(jnp.int32, (TILE, TILE), 1)
        return jnp.where(col <= row if lower else row <= col, 1.0, 0.0).astype(BF16)

    def query_mask(slot, t, first, last):
        mask = tile_mask(slot, t, first, last)
        if slot == 0:
            n = mask.shape[1] - TILE
            corner = mask[:, n:] * triangle(True)
            mask = jnp.concatenate([mask[:, :n], corner], axis=1) if n else corner
        return mask

    def key_mask(slot, t, first, last):
        mask = tile_mask(slot, t, first, last)
        if slot == 0:
            n = mask.shape[1] - TILE
            corner = mask[:, :TILE] * triangle(False)
            mask = jnp.concatenate([corner, mask[:, TILE:]], axis=1) if n else corner
        return mask

    def put(ref, rows, part, begin):
        ref[rows, :] = part if begin else ref[rows, :] + part

    def over_tiles(step, spans, tiles=range(ntile)):
        if spans is None:
            def body(t, carry):
                step(t, 0, ntile)
                return carry

            lax.fori_loop(0, ntile, body, 0)
        else:
            for t in tiles:
                step(t, *spans(t))

    def upto(t):
        return 0, t + 1

    def onward(t):
        return t, ntile

    def kept(bufs, j, shifted, rows, first, last):
        shift = 1 if j == shifted else 0
        cols = slice((first + shift) * TILE, (last + shift) * TILE)
        return bufs[j % 2].at[rows, cols]

    def attend(slot, spans, sums=True, slopes=True, tiles=range(ntile)):
        def step(t, first, last):
            rows = tile_rows(t)
            cols = slice(first * TILE, last * TILE)
            u = (dot_nt(qh[0, rows, :], kv[slot, cols, :DH]) * (0.5 * scale)).astype(BF16)
            w, slope2 = silu_parts(u, query_mask(slot, t, first, last))
            if sums:
                put(attn, rows, dot_nn(w, kv[slot, cols, DH:]), slot == 0)
            if slopes:
                kept(q_slopes, slot, 2, rows, first, last)[...] = slope2

        over_tiles(step, spans, tiles)

    def key_parts(j, spans):
        slot = 0 if j == 0 else 2 + j

        def step(t, first, last):
            rows = tile_rows(t)
            cols = slice(first * TILE, last * TILE)
            u = (dot_nt(kv[0, rows, :DH], qh[j, cols, :]) * (0.5 * scale)).astype(BF16)
            w, slope2 = silu_parts(u, key_mask(slot, t, first, last))
            kept(k_weights, j, 0, rows, first, last)[...] = w
            kept(k_slopes, j, 0, rows, first, last)[...] = slope2

        over_tiles(step, spans)

    block_masks(0)
    attend(0, upto)

    load_wo.wait()
    swap_c.wait_recv()

    def grad_mix(t, carry):
        rows = tile_rows(t)
        gm[rows, :] = dot_nn(cs[rows, :], wo[:, head_dh])
        return carry

    def hop(src, dst, start, size, device):
        rows = pl.ds(start, size)
        i = len(sent)
        copy = pltpu.make_async_remote_copy(
            src_ref=src.at[rows],
            dst_ref=dst.at[rows],
            send_sem=ssem.at[i],
            recv_sem=rsem.at[i],
            device_id=device,
            device_id_type=MESH,
        )
        sent.append(copy)
        return copy

    kv_lo = hop(kv.at[1], kv.at[2], BLK, half - BLK, at_chip(chip_next[0]))
    kv_hi = hop(kv.at[1], kv.at[2], half, half, at_chip(chip_next[0]))
    q_lo = hop(qh.at[1], qh.at[2], 0, half, at_chip(chip_prev[0]))
    q_hi = hop(qh.at[1], qh.at[2], half, half - BLK, at_chip(chip_prev[0]))
    kv[2, :BLK, :] = jnp.zeros((BLK, 2 * DH), BF16)
    qh[2, T - BLK :, :] = jnp.zeros((BLK, DH), BF16)
    dah[2, T - BLK :, :] = jnp.zeros((BLK, DH), BF16)

    def start_one(first, second):
        pl.when(r == 0)(first.start)
        pl.when(r == 1)(second.start)

    kv_a.wait_recv()
    start_one(kv_lo, kv_hi)
    q_a.wait_recv()
    start_one(q_lo, q_hi)

    lax.fori_loop(0, ntile, grad_mix, 0)
    lax.fori_loop(0, nblk, gates_and_slopes, 0)
    key_parts(0, onward)

    kv_b.wait_recv()
    start_one(kv_hi, kv_lo)
    q_b.wait_recv()
    start_one(q_hi, q_lo)
    for copy in id_copies:
        copy.wait_recv()
    for slot in range(1, 5):
        block_masks(slot)
    attend(1, None)

    def turn(b, carry):
        rows = pl.ds(pl.multiple_of(b * BLK, BLK), BLK)
        xt[:, rows] = xs[rows, :].T
        ct[:, rows] = cs[rows, :].T
        return carry

    lax.fori_loop(0, nblk, turn, 0)
    for h in range(2):
        for i, p in enumerate((0, 2, 1, 3)):
            wpp[:, (4 * h + i) * DH : (4 * h + i + 1) * DH] = wp[
                :, (4 * h + p) * DH : (4 * h + p + 1) * DH
            ]
    key_parts(1, None)
    kv_lo.wait_recv()
    kv_hi.wait_recv()

    lane = lax.broadcasted_iota(jnp.int32, (BLK, BLK), 1)
    quarter = half // 2

    def send_sums(h):
        for b in range(quarter // BLK):
            packed = []
            for e in range(2):
                rows = pl.ds(h * half + e * quarter + b * BLK, BLK)
                a = attn[rows, :]
                gn = gm[rows, :] * gate[rows, :].astype(F32)
                sums = [a, a * a, gn, gn * a]
                column = jnp.zeros((BLK, BLK), F32)
                for i, term in enumerate(sums):
                    total = jnp.sum(term, axis=1, keepdims=True)
                    column = jnp.where(lane == 4 * e + i, total, column)
                packed.append(column)
            stat[h, 0, :, b * BLK : (b + 1) * BLK] = (packed[0] + packed[1]).T[:8, :]
        return [
            push(stat.at[h, 0], stat.at[h, i + 1], device) for i, device in enumerate(group)
        ]

    def normalise(h, copies):
        for copy in copies:
            copy.wait_recv()
        total = stat[h, 0]
        for i in range(len(group)):
            total = total + stat[h, i + 1]
        derived = []
        for e in range(2):
            s1, s2, s3, s4 = [total[4 * e + i : 4 * e + i + 1, :] for i in range(4)]
            mean = s1 / D
            inv = lax.rsqrt(s2 / D - mean * mean + 1e-05)
            derived += [mean, inv, s3 / D, (s4 - mean * s3) * inv / D]
        derived = jnp.concatenate(derived, axis=0)
        for b in range(quarter // BLK):
            columns = jnp.concatenate(
                [derived[:, b * BLK : (b + 1) * BLK], jnp.zeros((BLK - 8, BLK), F32)], axis=0
            ).T
            for e in range(2):
                rows = pl.ds(h * half + e * quarter + b * BLK, BLK)
                mean, inv, mean_grad, mean_cross = [
                    columns[:, 4 * e + i : 4 * e + i + 1] for i in range(4)
                ]
                g = gate[rows, :].astype(F32)
                grad_mixed = gm[rows, :]
                normed = (attn[rows, :] - mean) * inv
                dah[0, rows, :] = (
                    (grad_mixed * g - mean_grad - normed * mean_cross) * inv
                ).astype(BF16)
                mx[rows, :] = (normed * g).astype(BF16)
                gpre[rows, :DH] = (grad_mixed * normed * slope[rows, :DH]).astype(BF16)
        rows = pl.ds(h * half, half)
        return push(dah.at[0, rows], dah.at[1, rows], at_chip(chip_prev[0]))

    low, high = range(ntile // 2), range(ntile // 2, ntile)
    attend(2, onward, slopes=False, tiles=low)
    low_sums = send_sums(0)
    attend(2, onward, slopes=False, tiles=high)
    high_sums = send_sums(1)
    attend(2, onward, sums=False, tiles=high)
    da_copies = [normalise(0, low_sums)]
    da_copies.append(normalise(1, high_sums))
    attend(2, onward, sums=False, tiles=low)

    swap_mx = push(mx.at[oth_rows], m2.at[:, head_dh], partner)
    m2[:, head_dh] = mx[own_rows, :]

    def query_grads(slot, spans):
        def step(t, first, last):
            rows = tile_rows(t)
            cols = slice(first * TILE, last * TILE)
            gw = dot_nt(dah[0, rows, :], kv[slot, cols, DH:]).astype(BF16)
            ds = gw * kept(q_slopes, slot, 2, rows, first, last)[...]
            put(dq, rows, dot_nn(ds, kv[slot, cols, :DH]), slot == 0)

        over_tiles(step, spans)

    def key_grads(j, spans):
        def step(t, first, last):
            rows = tile_rows(t)
            cols = slice(first * TILE, last * TILE)
            gw = dot_nt(kv[0, rows, DH:], dah[j, cols, :]).astype(BF16)
            ds = gw * kept(k_slopes, j, 0, rows, first, last)[...]
            w = kept(k_weights, j, 0, rows, first, last)[...]
            put(dv, rows, dot_nn(w, dah[j, cols, :]), j == 0)
            put(dk, rows, dot_nn(ds, qh[j, cols, :]), j == 0)

        over_tiles(step, spans)

    def ring_far(n, device, term, bufs, cols):
        send, far, near, last, own = bufs
        h = far.shape[0] // 2
        early, late = pl.ds(0, h), pl.ds(h, h)
        if n != 4:
            return []
        send[0, :, cols] = term(2).astype(BF16)
        return [
            push(send.at[0, early, cols], far.at[early, cols], device(1)),
            push(send.at[0, late, cols], far.at[late, cols], device(-1)),
        ]

    def ring_near(n, device, term, bufs, cols):
        send, far, near, last, own = bufs
        h = far.shape[0] // 2
        early, late = pl.ds(0, h), pl.ds(h, h)
        part = term(1)
        near[0, :, cols] = part[:h, :]
        send[1, late, cols] = part[h:, :].astype(BF16)
        copies = [push(send.at[1, late, cols], last.at[0, late, cols], device(1))]
        if n == 4:
            part = term(3)
            near[1, :, cols] = part[h:, :]
            send[2, early, cols] = part[:h, :].astype(BF16)
            copies.append(push(send.at[2, early, cols], last.at[1, early, cols], device(-1)))
        return copies

    def ring_own(term, bufs, cols):
        bufs[4][:, cols] = term(0)

    def ring_first(n, device, term, bufs, cols):
        copies = ring_far(n, device, term, bufs, cols)
        copies += ring_near(n, device, term, bufs, cols)
        ring_own(term, bufs, cols)
        return copies

    def ring_second(n, device, bufs, cols, copies):
        send, far, near, last, own = bufs
        h = far.shape[0] // 2
        early, late = pl.ds(0, h), pl.ds(h, h)
        out = copies[2:] if n == 4 else copies
        part = near[0, :, cols]
        if n == 4:
            copies[0].wait_recv()
            part = part + far[early, cols].astype(F32)
        send[1, early, cols] = part.astype(BF16)
        out.append(push(send.at[1, early, cols], last.at[0, early, cols], device(1)))
        if n == 4:
            copies[1].wait_recv()
            part = near[1, :, cols] + far[late, cols].astype(F32)
            send[2, late, cols] = part.astype(BF16)
            out.append(push(send.at[2, late, cols], last.at[1, late, cols], device(-1)))
        return out

    def ring_total(bufs, cols, copies):
        send, far, near, last, own = bufs
        for copy in copies:
            copy.wait_recv()
        part = own[:, cols]
        for i in range(len(copies) // 2):
            part = part + last[i, :, cols].astype(F32)
        return part

    def weight_term(lhs_t, rhs):
        def term(d):
            at = pl.multiple_of(lax.rem(y + d, ny) * RY, RY)
            return dot_nn(lhs_t[pl.ds(at, RY), :], rhs)

        return term

    def model_term(rows_ref, weight):
        def term(d):
            at = pl.multiple_of(lax.rem(x + d, nx) * CW, CW)
            return dot_nt(rows_ref[...], weight[pl.ds(at, CW), :])

        return term

    def over_z(cols, copies):
        part = ring_total(w_bufs, cols, copies)
        w_bufs[4][:, cols] = part
        w_s2[:, cols] = part.astype(BF16)
        later = []
        for dz in range(nz):
            for dr in range(2):
                if dz or dr:
                    side = lax.rem(r + dr, 2)
                    at = pl.multiple_of(lax.rem(z + dz, nz) * RZ + side * RC, RC)
                    later.append(
                        push(
                            w_s2.at[pl.ds(at, RC), cols],
                            w_r2.at[dr, dz, :, cols],
                            at_z(dz, dr),
                        )
                    )
        return later

    every = pl.ds(0, CW)
    early_cols, late_cols = pl.ds(0, 3 * DH), pl.ds(3 * DH, 2 * DH)

    q_lo.wait_recv()
    q_hi.wait_recv()
    query_grads(0, upto)
    swap_mx.wait_recv()
    lo_first = ring_first(nx, at_x, model_term(m2, wo), lo_bufs, every)
    da_copies[0].wait_recv()
    rows = pl.ds(0, half)
    da_fa = push(dah.at[1, rows], dah.at[2, rows], at_chip(chip_prev[0]))
    query_grads(1, None)
    da_copies[1].wait_recv()
    rows = pl.ds(half, half - BLK)
    da_fb = push(dah.at[1, rows], dah.at[2, rows], at_chip(chip_prev[0]))
    lo_second = ring_second(nx, at_x, lo_bufs, every, lo_first)
    query_grads(2, onward)
    gpre[:, DH : 2 * DH] = (
        dq[...] * mcol[...] * (0.5 * scale) * slope[:, 2 * DH : 3 * DH]
    ).astype(BF16)
    early = pl.ds(pl.multiple_of(r * 4 * DH, 4 * DH), 2 * DH)
    late = pl.ds(pl.multiple_of(r * 4 * DH + 2 * DH, 2 * DH), 2 * DH)
    swap_early = push(gpre.at[oth_rows, : 2 * DH], g2.at[:, early], partner)
    out_term = weight_term(ct, mx[...])
    query_term = weight_term(xt, gpre[:, : 2 * DH])

    def early_term(d):
        return jnp.concatenate([out_term(d), query_term(d)], axis=1)

    early_first = ring_first(ny, at_y, early_term, w_bufs, early_cols)
    key_grads(0, onward)
    early_second = ring_second(ny, at_y, w_bufs, early_cols, early_first)
    key_grads(1, None)
    early_z = over_z(early_cols, early_second)
    key_parts(2, upto)
    da_fa.wait_recv()
    da_fb.wait_recv()
    key_grads(2, upto)
    gpre[:, 2 * DH : 3 * DH] = (dv[...] * slope[:, DH : 2 * DH]).astype(BF16)
    gpre[:, 3 * DH :] = (dk[...] * mcol[...] * (0.5 * scale) * slope[:, 3 * DH :]).astype(BF16)
    settled = len(sent)
    swap_late = push(gpre.at[oth_rows, 2 * DH :], g2.at[:, late], partner)
    g2[:, head_cols] = gpre[own_rows, :]
    late_term = weight_term(xt, gpre[:, 2 * DH :])
    gi_term = model_term(g2, wpp)
    late_first = ring_far(ny, at_y, late_term, w_bufs, late_cols)
    swap_early.wait_recv()
    swap_late.wait_recv()
    gi_first = ring_far(nx, at_x, gi_term, gi_bufs, every)
    late_first += ring_near(ny, at_y, late_term, w_bufs, late_cols)
    gi_first += ring_near(nx, at_x, gi_term, gi_bufs, every)
    ring_own(late_term, w_bufs, late_cols)
    late_second = ring_second(ny, at_y, w_bufs, late_cols, late_first)
    gi_second = ring_second(nx, at_x, gi_bufs, every, gi_first)
    ring_own(gi_term, gi_bufs, every)
    late_z = over_z(late_cols, late_second)

    model_cols = pl.ds(pl.multiple_of(x * CW, CW), CW)
    lo = ring_total(lo_bufs, every, lo_second)
    lo_ref[...] = (xs[own_rows, model_cols].astype(F32) + lo).astype(BF16)

    for copy in sent[:settled]:
        copy.wait_send()
    for copy in early_z + late_z:
        copy.wait_recv()
    own_part = w_bufs[4][pl.ds(pl.multiple_of(z * RZ + r * RC, RC), RC), :]
    for dr in range(2):
        part = own_part if dr == 0 else w_r2[1, 0].astype(F32)
        for dz in range(1, nz):
            part = part + w_r2[dr, dz].astype(F32)
        part = part * grad_scale
        side = lax.rem(r + dr, 2)
        go_ref[:, pl.ds(pl.multiple_of(side * DH, DH), DH)] = part[:, :DH]
        for p, i in enumerate((1, 3, 2, 4)):
            cols = pl.ds(pl.multiple_of(side * 4 * DH + p * DH, DH), DH)
            gp_ref[:, cols] = part[:, i * DH : (i + 1) * DH]

    gi = ring_total(gi_bufs, every, gi_second)
    gi_ref[...] = (cs[own_rows, model_cols].astype(F32) + gi).astype(BF16)

    for copy in sent[settled:]:
        copy.wait_send()


def hand_on(*refs):
    n = len(refs) // 2
    for src, dst in zip(refs[:n], refs[n:]):
        dst[...] = src[...]


def body(nx, ny, nz, inputs, proj_weight, out_weight, cotangent, block_history, event_mask):
    half, D = inputs.shape
    T = 2 * half
    CW = D // nx
    RY = D // ny
    RZ = RY // nz
    nblk = half // BLK
    vmem = pl.BlockSpec(memory_space=pltpu.VMEM)
    hbm = pl.BlockSpec(memory_space=pltpu.HBM)
    V = pltpu.VMEM

    def ring_bufs(rows, cols):
        return (
            V((3, rows, cols), BF16),
            V((rows, cols), BF16),
            V((2, rows // 2, cols), F32),
            V((2, rows, cols), BF16),
            V((rows, cols), F32),
        )

    def pair_bufs():
        return V((T, T + TILE), BF16), V((T, T), BF16)

    out_shape = (
        jax.ShapeDtypeStruct((half, CW), BF16),
        jax.ShapeDtypeStruct((half, CW), BF16),
        jax.ShapeDtypeStruct((RZ // 2, 8 * DH), F32),
        jax.ShapeDtypeStruct((RZ // 2, 2 * DH), F32),
    )
    results = pl.pallas_call(
        functools.partial(layer_kernel, nx, ny, nz, half * 2 * ny * nz),
        out_shape=out_shape,
        in_specs=[hbm] * 4 + [pl.BlockSpec(memory_space=pltpu.SMEM), vmem],
        out_specs=(vmem,) * 4,
        scratch_shapes=[
            V((D, 8 * DH), BF16),
            V((D, 2 * DH), BF16),
            V((D, 8 * DH), BF16),
            V((T, D), BF16),
            V((T, D), BF16),
            V((D, T), BF16),
            V((D, T), BF16),
            V((2, 8, BLK), jnp.int32),
            V((5, 8, BLK), jnp.int32),
            V((5, 8, T), F32),
            V((T, DH), F32),
            V((T, 4 * DH), F32),
            V((T, DH), BF16),
            V((3, T, 2 * DH), BF16),
            V((3, T, DH), BF16),
            V((3, T, DH), BF16),
            V((T, DH), F32),
            V((T, DH), F32),
            V((2, 2 * nx, 8, half // 2), F32),
            V((T, DH), BF16),
            V((half, 2 * DH), BF16),
            V((T, 4 * DH), BF16),
            V((half, 8 * DH), BF16),
            V((T, DH), F32),
            V((T, DH), F32),
            V((T, DH), F32),
            ring_bufs(half, CW),
            ring_bufs(half, CW),
            ring_bufs(RY, 5 * DH),
            V((RY, 5 * DH), BF16),
            V((2, nz, RZ // 2, 5 * DH), BF16),
            pair_bufs(),
            pair_bufs(),
            pair_bufs(),
            pltpu.SemaphoreType.DMA((4,)),
            pltpu.SemaphoreType.DMA((MAX_COPIES,)),
            pltpu.SemaphoreType.DMA((MAX_COPIES,)),
        ],
        compiler_params=pltpu.CompilerParams(
            collective_id=0, has_side_effects=True, vmem_limit_bytes=60 * 1024 * 1024
        ),
    )(
        inputs,
        proj_weight,
        out_weight,
        cotangent,
        block_history,
        event_mask.reshape(nblk, BLK),
    )
    return pl.pallas_call(
        hand_on,
        out_shape=out_shape,
        in_specs=[vmem] * 4,
        out_specs=(vmem,) * 4,
    )(*results)


def solution(mesh):
    nx = mesh.shape["head"]
    chips = mesh.shape["seq"] // 2
    nz = 8 if chips % 32 == 0 else 2
    ny = chips // nz
    return jax.shard_map(
        functools.partial(body, nx, ny, nz),
        mesh=mesh,
        in_specs=(
            P("seq", None),
            P(None, "head"),
            P(None, "head"),
            P("seq", None),
            P("seq"),
            P("seq"),
        ),
        out_specs=(P("seq", "head"), P("seq", "head"), P("seq", "head"), P("seq", "head")),
        check_vma=False,
    )
```

```python
import functools

import jax
import jax.numpy as jnp
from jax import lax
from jax.experimental import pallas as pl
from jax.experimental.pallas import tpu as pltpu
from jax.sharding import PartitionSpec as P

MESH = pl.DeviceIdType.MESH
DH = 128
BLK = 128
TILE = 256
F32 = jnp.float32
BF16 = jnp.bfloat16
NT = (((1,), (1,)), ((), ()))
MAX_COPIES = 128


def dot_nt(a, b):
    return lax.dot_general(a, b, NT, preferred_element_type=F32)


def dot_nn(a, b):
    return jnp.dot(a, b, preferred_element_type=F32)


def silu_parts(u, mask):
    t = jnp.tanh(u)
    p = 1.0 + t
    if mask is not None:
        p = p * mask
    w = u * p
    return w, p + w * (1.0 - t)


def layer_kernel(
    nx,
    ny,
    nz,
    token_total,
    inp,
    wp_hbm,
    wo_hbm,
    cot,
    history,
    events,
    lo_ref,
    gi_ref,
    gp_ref,
    go_ref,
    wo,
    wpp,
    xs,
    cs,
    xt,
    mxt,
    metas,
    ids,
    mk,
    mcol,
    slope,
    gate,
    kv,
    qh,
    dah,
    attn,
    gm,
    stat,
    mx,
    m2,
    gpre,
    g2,
    dq,
    dk,
    dv,
    lo_bufs,
    gi_bufs,
    w_bufs,
    w_s2,
    w_r2,
    q_slopes,
    k_weights,
    k_slopes,
    lsem,
    ssem,
    rsem,
):
    s = lax.axis_index("seq")
    x = lax.axis_index("head")
    r = lax.rem(s, 2)
    o = 1 - r
    c = s // 2
    nc = ny * nz
    z = lax.rem(c, nz)
    y = c // nz
    half = inp.shape[0]
    T = 2 * half
    D = inp.shape[1]
    CW = D // nx
    RY = D // ny
    RZ = RY // nz
    RC = RZ // 2
    nblk = T // BLK
    ntile = T // TILE
    scale = DH ** (-0.5)
    grad_scale = token_total ** (-0.5)

    own0 = pl.multiple_of(r * half, half)
    oth0 = pl.multiple_of(o * half, half)
    own_rows = pl.ds(own0, half)
    oth_rows = pl.ds(oth0, half)
    head_cols = pl.ds(pl.multiple_of(r * 4 * DH, 4 * DH), 4 * DH)
    gq_cols = pl.ds(pl.multiple_of(r * 4 * DH, 2 * DH), 2 * DH)
    kv_cols = pl.ds(pl.multiple_of(r * 4 * DH + 2 * DH, 2 * DH), 2 * DH)
    head_dh = pl.ds(pl.multiple_of(r * DH, DH), DH)

    def load_group(head, first, sems):
        copies = []
        for i in (first, first + 1):
            src = pl.ds(pl.multiple_of(head * 4 * DH + (0, 2, 1, 3)[i] * DH, DH), DH)
            dst = pl.ds(pl.multiple_of(head * 4 * DH + i * DH, DH), DH)
            copies.append(
                pltpu.make_async_copy(wp_hbm.at[:, src], wpp.at[:, dst], lsem.at[sems + i - first])
            )
        return copies

    load_x = pltpu.make_async_copy(inp, xs.at[own_rows], lsem.at[0])
    load_c = pltpu.make_async_copy(cot, cs.at[own_rows], lsem.at[1])
    load_wo = pltpu.make_async_copy(wo_hbm, wo, lsem.at[2])
    load_kv = load_group(r, 2, 3)
    load_gq = load_group(r, 0, 5)
    load_rest = load_group(o, 0, 7) + load_group(o, 2, 9)
    for copy in [load_x] + load_kv + load_gq + [load_c, load_wo] + load_rest:
        copy.start()

    def at_chip(chip):
        return (chip * 2 + r, x)

    chip_next = [lax.rem(c + d, nc) for d in (1, 2)]
    chip_prev = [lax.rem(c + nc - d, nc) for d in (1, 2)]
    partner = (c * 2 + o, x)

    def at_x(dx):
        return (s, lax.rem(x + nx + dx, nx))

    def at_y(dy):
        return at_chip(lax.rem(y + ny + dy, ny) * nz + z)

    def at_z(dz, dr):
        chip = y * nz + lax.rem(z + dz, nz)
        return (chip * 2 + lax.rem(r + dr, 2), x)

    group = []
    for dx in range(nx):
        for dr in range(2):
            if dx or dr:
                group.append((c * 2 + lax.rem(r + dr, 2), lax.rem(x + dx, nx)))
    peers = list(group)
    peers += [at_chip(k) for k in chip_next + chip_prev]
    peers += [at_y(d) for d in ((1, -1) if ny > 2 else (1,))]
    peers += [at_z(d, e) for d in range(1, nz) for e in range(2)]

    barrier = pltpu.get_barrier_semaphore()
    for peer in peers:
        pl.semaphore_signal(barrier, inc=1, device_id=peer, device_id_type=MESH)

    sent = []

    def push(src, dst, device):
        i = len(sent)
        copy = pltpu.make_async_remote_copy(
            src_ref=src,
            dst_ref=dst,
            send_sem=ssem.at[i],
            recv_sem=rsem.at[i],
            device_id=device,
            device_id_type=MESH,
        )
        copy.start()
        sent.append(copy)
        return copy

    def mask_columns(block_meta, row0):
        for b in range(nblk // 2):
            row = block_meta[4 + b : 5 + b, :].astype(F32)
            mcol[pl.ds(row0 + b * BLK, BLK), :] = jnp.broadcast_to(row, (BLK, BLK)).T

    def project_kv(row0):
        def step(t, carry):
            rows = pl.ds(pl.multiple_of(row0 + t * TILE, TILE), TILE)
            u = dot_nn(xs[rows, :], wpp[:, kv_cols]) * 0.5
            slope[rows, 2 * DH :] = u
            act = u * (1.0 + jnp.tanh(u))
            kv[0, rows, DH:] = act[:, :DH].astype(BF16)
            kv[0, rows, :DH] = (act[:, DH:] * mcol[rows, :]).astype(BF16)
            return carry

        lax.fori_loop(0, half // TILE, step, 0)

    def project_gq(row0):
        def step(t, carry):
            rows = pl.ds(pl.multiple_of(row0 + t * TILE, TILE), TILE)
            u = dot_nn(xs[rows, :], wpp[:, gq_cols]) * 0.5
            slope[rows, : 2 * DH] = u
            u = u[:, DH:]
            qh[0, rows, :] = (u * (1.0 + jnp.tanh(u)) * mcol[rows, :]).astype(BF16)
            return carry

        lax.fori_loop(0, half // TILE, step, 0)

    def gates_and_slopes(t, carry):
        rows = pl.ds(pl.multiple_of(t * BLK, BLK), BLK)
        act, slope2 = silu_parts(slope[rows, :], None)
        gate[rows, :] = act[:, :DH].astype(BF16)
        slope[rows, :] = 0.5 * slope2
        return carry

    own_meta = jnp.concatenate(
        [jnp.full((1, BLK), history[b], jnp.int32) for b in range(nblk // 2)] + [events[...]],
        axis=0,
    )
    metas[r] = own_meta
    mask_columns(own_meta, own0)
    load_x.wait()
    for copy in load_kv:
        copy.wait()
    project_kv(own0)

    pl.semaphore_wait(barrier, len(peers))
    kv_a = push(kv.at[0, own_rows], kv.at[1, own_rows], at_chip(chip_next[0]))
    swap_x = push(xs.at[own_rows], xs.at[own_rows], partner)
    swap_meta = push(metas.at[r], metas.at[r], partner)
    for copy in load_gq:
        copy.wait()
    project_gq(own0)
    q_a = push(qh.at[0, own_rows], qh.at[1, own_rows], at_chip(chip_prev[0]))
    load_c.wait()
    swap_c = push(cs.at[own_rows], cs.at[own_rows], partner)

    def turn(b, carry):
        rows = pl.ds(pl.multiple_of(b * BLK, BLK), BLK)
        xt[:, rows] = xs[rows, :].T
        return carry

    lax.fori_loop(r * (nblk // 2), (r + 1) * (nblk // 2), gates_and_slopes, 0)
    lax.fori_loop(r * (nblk // 2), (r + 1) * (nblk // 2), turn, 0)
    swap_meta.wait_recv()
    mask_columns(metas[o], oth0)
    swap_x.wait_recv()
    project_kv(oth0)
    kv_b = push(kv.at[0, oth_rows], kv.at[1, oth_rows], at_chip(chip_next[0]))
    project_gq(oth0)
    q_b = push(qh.at[0, oth_rows], qh.at[1, oth_rows], at_chip(chip_prev[0]))

    ids[0] = jnp.concatenate([metas[0][:4], metas[1][:4]], axis=0)
    id_copies = [
        push(ids.at[0], ids.at[1], at_chip(chip_next[0])),
        push(ids.at[0], ids.at[2], at_chip(chip_next[1])),
        push(ids.at[0], ids.at[3], at_chip(chip_prev[0])),
        push(ids.at[0], ids.at[4], at_chip(chip_prev[1])),
    ]

    def block_masks(slot):
        own = ids[0]
        other = ids[slot]
        for k in range(nblk):
            same = jnp.broadcast_to(other[k : k + 1, :], own.shape) == own
            mk[slot, :, k * BLK : (k + 1) * BLK] = jnp.where(same, 1.0, 0.0)

    def tile_rows(t):
        return pl.ds(t * TILE if isinstance(t, int) else pl.multiple_of(t * TILE, TILE), TILE)

    def tile_mask(slot, t, first, last):
        cols = slice(first * TILE, last * TILE)
        n = (last - first) * TILE
        return jnp.concatenate(
            [
                jnp.broadcast_to(
                    mk[slot, pl.ds((TILE // BLK) * t + i, 1), cols].astype(BF16), (BLK, n)
                )
                for i in range(TILE // BLK)
            ],
            axis=0,
        )

    def triangle(lower):
        row = lax.broadcasted_iota(jnp.int32, (TILE, TILE), 0)
        col = lax.broadcasted_iota(jnp.int32, (TILE, TILE), 1)
        return jnp.where(col <= row if lower else row <= col, 1.0, 0.0).astype(BF16)

    def query_mask(slot, t, first, last):
        mask = tile_mask(slot, t, first, last)
        if slot == 0:
            n = mask.shape[1] - TILE
            corner = mask[:, n:] * triangle(True)
            mask = jnp.concatenate([mask[:, :n], corner], axis=1) if n else corner
        return mask

    def key_mask(slot, t, first, last):
        mask = tile_mask(slot, t, first, last)
        if slot == 0:
            n = mask.shape[1] - TILE
            corner = mask[:, :TILE] * triangle(False)
            mask = jnp.concatenate([corner, mask[:, TILE:]], axis=1) if n else corner
        return mask

    def put(ref, rows, part, begin):
        ref[rows, :] = part if begin else ref[rows, :] + part

    def over_tiles(step, spans, tiles=range(ntile)):
        if spans is None:
            def body(t, carry):
                step(t, 0, ntile)
                return carry

            lax.fori_loop(0, ntile, body, 0)
        else:
            for t in tiles:
                step(t, *spans(t))

    def upto(t):
        return 0, t + 1

    def onward(t):
        return t, ntile

    def kept(bufs, j, shifted, rows, first, last):
        shift = 1 if j == shifted else 0
        cols = slice((first + shift) * TILE, (last + shift) * TILE)
        return bufs[j % 2].at[rows, cols]

    def attend(slot, spans, tiles=range(ntile)):
        def step(t, first, last):
            rows = tile_rows(t)
            cols = slice(first * TILE, last * TILE)
            u = (dot_nt(qh[0, rows, :], kv[slot, cols, :DH]) * (0.5 * scale)).astype(BF16)
            w, slope2 = silu_parts(u, query_mask(slot, t, first, last))
            put(attn, rows, dot_nn(w, kv[slot, cols, DH:]), slot == 0)
            kept(q_slopes, slot, 2, rows, first, last)[...] = slope2

        over_tiles(step, spans, tiles)

    def key_parts(j, spans):
        slot = 0 if j == 0 else 2 + j

        def step(t, first, last):
            rows = tile_rows(t)
            cols = slice(first * TILE, last * TILE)
            u = (dot_nt(kv[0, rows, :DH], qh[j, cols, :]) * (0.5 * scale)).astype(BF16)
            w, slope2 = silu_parts(u, key_mask(slot, t, first, last))
            kept(k_weights, j, 0, rows, first, last)[...] = w
            kept(k_slopes, j, 0, rows, first, last)[...] = slope2

        over_tiles(step, spans)

    block_masks(0)
    attend(0, upto)

    load_wo.wait()
    for copy in load_rest:
        copy.wait()
    swap_c.wait_recv()

    def grad_mix(t, carry):
        rows = tile_rows(t)
        gm[rows, :] = dot_nn(cs[rows, :], wo[:, head_dh])
        return carry

    def hop(src, dst, start, size, device):
        rows = pl.ds(start, size)
        i = len(sent)
        copy = pltpu.make_async_remote_copy(
            src_ref=src.at[rows],
            dst_ref=dst.at[rows],
            send_sem=ssem.at[i],
            recv_sem=rsem.at[i],
            device_id=device,
            device_id_type=MESH,
        )
        sent.append(copy)
        return copy

    kv_lo = hop(kv.at[1], kv.at[2], BLK, half - BLK, at_chip(chip_next[0]))
    kv_hi = hop(kv.at[1], kv.at[2], half, half, at_chip(chip_next[0]))
    q_lo = hop(qh.at[1], qh.at[2], 0, half, at_chip(chip_prev[0]))
    q_hi = hop(qh.at[1], qh.at[2], half, half - BLK, at_chip(chip_prev[0]))
    kv[2, :BLK, :] = jnp.zeros((BLK, 2 * DH), BF16)
    qh[2, T - BLK :, :] = jnp.zeros((BLK, DH), BF16)
    dah[2, T - BLK :, :] = jnp.zeros((BLK, DH), BF16)

    def start_one(first, second):
        pl.when(r == 0)(first.start)
        pl.when(r == 1)(second.start)

    kv_a.wait_recv()
    start_one(kv_lo, kv_hi)
    q_a.wait_recv()
    start_one(q_lo, q_hi)

    lax.fori_loop(0, ntile, grad_mix, 0)
    lax.fori_loop(o * (nblk // 2), (o + 1) * (nblk // 2), gates_and_slopes, 0)
    key_parts(0, onward)

    kv_b.wait_recv()
    start_one(kv_hi, kv_lo)
    q_b.wait_recv()
    start_one(q_hi, q_lo)
    for copy in id_copies:
        copy.wait_recv()
    for slot in range(1, 5):
        block_masks(slot)
    attend(1, None)

    lax.fori_loop(o * (nblk // 2), (o + 1) * (nblk // 2), turn, 0)
    key_parts(1, None)
    kv_lo.wait_recv()
    kv_hi.wait_recv()

    lane = lax.broadcasted_iota(jnp.int32, (BLK, BLK), 1)
    quarter = half // 2

    def send_sums(h):
        for b in range(quarter // BLK):
            packed = []
            for e in range(2):
                rows = pl.ds(h * half + e * quarter + b * BLK, BLK)
                a = attn[rows, :]
                gn = gm[rows, :] * gate[rows, :].astype(F32)
                sums = [a, a * a, gn, gn * a]
                column = jnp.zeros((BLK, BLK), F32)
                for i, term in enumerate(sums):
                    total = jnp.sum(term, axis=1, keepdims=True)
                    column = jnp.where(lane == 4 * e + i, total, column)
                packed.append(column)
            stat[h, 0, :, b * BLK : (b + 1) * BLK] = (packed[0] + packed[1]).T[:8, :]
        return [
            push(stat.at[h, 0], stat.at[h, i + 1], device) for i, device in enumerate(group)
        ]

    def normalise(h, copies):
        for copy in copies:
            copy.wait_recv()
        total = stat[h, 0]
        for i in range(len(group)):
            total = total + stat[h, i + 1]
        derived = []
        for e in range(2):
            s1, s2, s3, s4 = [total[4 * e + i : 4 * e + i + 1, :] for i in range(4)]
            mean = s1 / D
            inv = lax.rsqrt(s2 / D - mean * mean + 1e-05)
            derived += [mean, inv, s3 / D, (s4 - mean * s3) * inv / D]
        derived = jnp.concatenate(derived, axis=0)
        for b in range(quarter // BLK):
            columns = jnp.concatenate(
                [derived[:, b * BLK : (b + 1) * BLK], jnp.zeros((BLK - 8, BLK), F32)], axis=0
            ).T
            for e in range(2):
                rows = pl.ds(h * half + e * quarter + b * BLK, BLK)
                mean, inv, mean_grad, mean_cross = [
                    columns[:, 4 * e + i : 4 * e + i + 1] for i in range(4)
                ]
                g = gate[rows, :].astype(F32)
                grad_mixed = gm[rows, :]
                normed = (attn[rows, :] - mean) * inv
                dah[0, rows, :] = (
                    (grad_mixed * g - mean_grad - normed * mean_cross) * inv
                ).astype(BF16)
                mx[rows, :] = (normed * g).astype(BF16)
                gpre[rows, :DH] = (grad_mixed * normed * slope[rows, :DH]).astype(BF16)
        rows = pl.ds(h * half, half)
        return push(dah.at[0, rows], dah.at[1, rows], at_chip(chip_prev[0]))

    low, high = range(ntile // 2), range(ntile // 2, ntile)
    attend(2, onward, tiles=low)
    low_sums = send_sums(0)
    attend(2, onward, tiles=high)
    high_sums = send_sums(1)
    q_lo.wait_recv()
    q_hi.wait_recv()
    key_parts(2, upto)
    da_early = normalise(0, low_sums)
    da_late = normalise(1, high_sums)

    swap_mx = push(mx.at[oth_rows], m2.at[:, head_dh], partner)
    m2[:, head_dh] = mx[own_rows, :]

    def query_grads(slot, spans):
        def step(t, first, last):
            rows = tile_rows(t)
            cols = slice(first * TILE, last * TILE)
            gw = dot_nt(dah[0, rows, :], kv[slot, cols, DH:]).astype(BF16)
            ds = gw * kept(q_slopes, slot, 2, rows, first, last)[...]
            put(dq, rows, dot_nn(ds, kv[slot, cols, :DH]), slot == 0)

        over_tiles(step, spans)

    def key_grads(j, spans):
        def step(t, first, last):
            rows = tile_rows(t)
            cols = slice(first * TILE, last * TILE)
            gw = dot_nt(kv[0, rows, DH:], dah[j, cols, :]).astype(BF16)
            ds = gw * kept(k_slopes, j, 0, rows, first, last)[...]
            w = kept(k_weights, j, 0, rows, first, last)[...]
            put(dv, rows, dot_nn(w, dah[j, cols, :]), j == 0)
            put(dk, rows, dot_nn(ds, qh[j, cols, :]), j == 0)

        over_tiles(step, spans)

    def ring_far(n, device, term, bufs, cols):
        send, far, near, last, own = bufs
        h = far.shape[0] // 2
        early, late = pl.ds(0, h), pl.ds(h, h)
        if n != 4:
            return []
        send[0, :, cols] = term(2).astype(BF16)
        return [
            push(send.at[0, early, cols], far.at[early, cols], device(1)),
            push(send.at[0, late, cols], far.at[late, cols], device(-1)),
        ]

    def ring_near(n, device, term, bufs, cols):
        send, far, near, last, own = bufs
        h = far.shape[0] // 2
        early, late = pl.ds(0, h), pl.ds(h, h)
        part = term(1)
        near[0, :, cols] = part[:h, :]
        send[1, late, cols] = part[h:, :].astype(BF16)
        copies = [push(send.at[1, late, cols], last.at[0, late, cols], device(1))]
        if n == 4:
            part = term(3)
            near[1, :, cols] = part[h:, :]
            send[2, early, cols] = part[:h, :].astype(BF16)
            copies.append(push(send.at[2, early, cols], last.at[1, early, cols], device(-1)))
        return copies

    def ring_own(term, bufs, cols):
        bufs[4][:, cols] = term(0)

    def ring_first(n, device, term, bufs, cols):
        copies = ring_far(n, device, term, bufs, cols)
        copies += ring_near(n, device, term, bufs, cols)
        ring_own(term, bufs, cols)
        return copies

    def ring_second(n, device, bufs, cols, copies):
        send, far, near, last, own = bufs
        h = far.shape[0] // 2
        early, late = pl.ds(0, h), pl.ds(h, h)
        out = copies[2:] if n == 4 else copies
        part = near[0, :, cols]
        if n == 4:
            copies[0].wait_recv()
            part = part + far[early, cols].astype(F32)
        send[1, early, cols] = part.astype(BF16)
        out.append(push(send.at[1, early, cols], last.at[0, early, cols], device(1)))
        if n == 4:
            copies[1].wait_recv()
            part = near[1, :, cols] + far[late, cols].astype(F32)
            send[2, late, cols] = part.astype(BF16)
            out.append(push(send.at[2, late, cols], last.at[1, late, cols], device(-1)))
        return out

    def ring_total(bufs, cols, copies):
        send, far, near, last, own = bufs
        for copy in copies:
            copy.wait_recv()
        part = own[:, cols]
        for i in range(len(copies) // 2):
            part = part + last[i, :, cols].astype(F32)
        return part

    def weight_term(lhs_t, rhs):
        def term(d):
            at = pl.multiple_of(lax.rem(y + d, ny) * RY, RY)
            return dot_nn(lhs_t[pl.ds(at, RY), :], rhs)

        return term

    def model_term(rows_ref, weight):
        def term(d):
            at = pl.multiple_of(lax.rem(x + d, nx) * CW, CW)
            return dot_nt(rows_ref[...], weight[pl.ds(at, CW), :])

        return term

    def over_z(cols, copies):
        part = ring_total(w_bufs, cols, copies)
        w_bufs[4][:, cols] = part
        w_s2[:, cols] = part.astype(BF16)
        later = []
        for dz in range(nz):
            for dr in range(2):
                if dz or dr:
                    side = lax.rem(r + dr, 2)
                    at = pl.multiple_of(lax.rem(z + dz, nz) * RZ + side * RC, RC)
                    later.append(
                        push(
                            w_s2.at[pl.ds(at, RC), cols],
                            w_r2.at[dr, dz, :, cols],
                            at_z(dz, dr),
                        )
                    )
        return later

    every = pl.ds(0, CW)
    early_cols, late_cols = pl.ds(0, 3 * DH), pl.ds(3 * DH, 2 * DH)

    query_grads(0, upto)
    swap_mx.wait_recv()
    lo_first = ring_first(nx, at_x, model_term(m2, wo), lo_bufs, every)
    da_early.wait_recv()
    rows = pl.ds(0, half)
    da_fa = push(dah.at[1, rows], dah.at[2, rows], at_chip(chip_prev[0]))
    query_grads(1, None)
    da_late.wait_recv()
    rows = pl.ds(half, half - BLK)
    da_fb = push(dah.at[1, rows], dah.at[2, rows], at_chip(chip_prev[0]))
    lo_second = ring_second(nx, at_x, lo_bufs, every, lo_first)
    query_grads(2, onward)
    gpre[:, DH : 2 * DH] = (
        dq[...] * mcol[...] * (0.5 * scale) * slope[:, DH : 2 * DH]
    ).astype(BF16)
    early = pl.ds(pl.multiple_of(r * 4 * DH, 4 * DH), 2 * DH)
    late = pl.ds(pl.multiple_of(r * 4 * DH + 2 * DH, 2 * DH), 2 * DH)
    swap_early = push(gpre.at[oth_rows, : 2 * DH], g2.at[:, early], partner)
    for b in range(nblk):
        mxt[:, b * BLK : (b + 1) * BLK] = mx[b * BLK : (b + 1) * BLK, :].T

    def out_term(d):
        at = pl.multiple_of(lax.rem(y + d, ny) * RY, RY)
        return dot_nn(mxt[...], cs[:, pl.ds(at, RY)]).T

    query_term = weight_term(xt, gpre[:, : 2 * DH])

    def early_term(d):
        return jnp.concatenate([out_term(d), query_term(d)], axis=1)

    early_first = ring_first(ny, at_y, early_term, w_bufs, early_cols)
    key_grads(0, onward)
    early_second = ring_second(ny, at_y, w_bufs, early_cols, early_first)
    key_grads(1, None)
    early_z = over_z(early_cols, early_second)
    da_fa.wait_recv()
    da_fb.wait_recv()
    key_grads(2, upto)
    gpre[:, 2 * DH : 3 * DH] = (dv[...] * slope[:, 2 * DH : 3 * DH]).astype(BF16)
    gpre[:, 3 * DH :] = (dk[...] * mcol[...] * (0.5 * scale) * slope[:, 3 * DH :]).astype(BF16)
    settled = len(sent)
    swap_late = push(gpre.at[oth_rows, 2 * DH :], g2.at[:, late], partner)
    g2[:, head_cols] = gpre[own_rows, :]
    late_term = weight_term(xt, gpre[:, 2 * DH :])
    gi_term = model_term(g2, wpp)
    late_first = ring_far(ny, at_y, late_term, w_bufs, late_cols)
    swap_early.wait_recv()
    swap_late.wait_recv()
    gi_first = ring_far(nx, at_x, gi_term, gi_bufs, every)
    late_first += ring_near(ny, at_y, late_term, w_bufs, late_cols)
    gi_first += ring_near(nx, at_x, gi_term, gi_bufs, every)
    ring_own(late_term, w_bufs, late_cols)
    late_second = ring_second(ny, at_y, w_bufs, late_cols, late_first)
    gi_second = ring_second(nx, at_x, gi_bufs, every, gi_first)
    ring_own(gi_term, gi_bufs, every)
    late_z = over_z(late_cols, late_second)

    model_cols = pl.ds(pl.multiple_of(x * CW, CW), CW)
    lo = ring_total(lo_bufs, every, lo_second)
    lo_ref[...] = (xs[own_rows, model_cols].astype(F32) + lo).astype(BF16)

    for copy in sent[:settled]:
        copy.wait_send()
    for copy in early_z + late_z:
        copy.wait_recv()
    own_part = w_bufs[4][pl.ds(pl.multiple_of(z * RZ + r * RC, RC), RC), :]
    for dr in range(2):
        part = own_part if dr == 0 else w_r2[1, 0].astype(F32)
        for dz in range(1, nz):
            part = part + w_r2[dr, dz].astype(F32)
        part = part * grad_scale
        side = lax.rem(r + dr, 2)
        go_ref[:, pl.ds(pl.multiple_of(side * DH, DH), DH)] = part[:, :DH]
        for p, i in enumerate((1, 3, 2, 4)):
            cols = pl.ds(pl.multiple_of(side * 4 * DH + p * DH, DH), DH)
            gp_ref[:, cols] = part[:, i * DH : (i + 1) * DH]

    gi = ring_total(gi_bufs, every, gi_second)
    gi_ref[...] = (cs[own_rows, model_cols].astype(F32) + gi).astype(BF16)

    for copy in sent[settled:]:
        copy.wait_send()


def hand_on(*refs):
    n = len(refs) // 2
    for src, dst in zip(refs[:n], refs[n:]):
        dst[...] = src[...]


def body(nx, ny, nz, inputs, proj_weight, out_weight, cotangent, block_history, event_mask):
    half, D = inputs.shape
    T = 2 * half
    CW = D // nx
    RY = D // ny
    RZ = RY // nz
    nblk = half // BLK
    vmem = pl.BlockSpec(memory_space=pltpu.VMEM)
    hbm = pl.BlockSpec(memory_space=pltpu.HBM)
    V = pltpu.VMEM

    def ring_bufs(rows, cols):
        return (
            V((3, rows, cols), BF16),
            V((rows, cols), BF16),
            V((2, rows // 2, cols), F32),
            V((2, rows, cols), BF16),
            V((rows, cols), F32),
        )

    def pair_bufs():
        return V((T, T + TILE), BF16), V((T, T), BF16)

    out_shape = (
        jax.ShapeDtypeStruct((half, CW), BF16),
        jax.ShapeDtypeStruct((half, CW), BF16),
        jax.ShapeDtypeStruct((RZ // 2, 8 * DH), F32),
        jax.ShapeDtypeStruct((RZ // 2, 2 * DH), F32),
    )
    results = pl.pallas_call(
        functools.partial(layer_kernel, nx, ny, nz, half * 2 * ny * nz),
        out_shape=out_shape,
        in_specs=[hbm] * 4 + [pl.BlockSpec(memory_space=pltpu.SMEM), vmem],
        out_specs=(vmem,) * 4,
        scratch_shapes=[
            V((D, 2 * DH), BF16),
            V((D, 8 * DH), BF16),
            V((T, D), BF16),
            V((T, D), BF16),
            V((D, T), BF16),
            V((DH, T), BF16),
            V((2, 8, BLK), jnp.int32),
            V((5, 8, BLK), jnp.int32),
            V((5, 8, T), F32),
            V((T, DH), F32),
            V((T, 4 * DH), F32),
            V((T, DH), BF16),
            V((3, T, 2 * DH), BF16),
            V((3, T, DH), BF16),
            V((3, T, DH), BF16),
            V((T, DH), F32),
            V((T, DH), F32),
            V((2, 2 * nx, 8, half // 2), F32),
            V((T, DH), BF16),
            V((half, 2 * DH), BF16),
            V((T, 4 * DH), BF16),
            V((half, 8 * DH), BF16),
            V((T, DH), F32),
            V((T, DH), F32),
            V((T, DH), F32),
            ring_bufs(half, CW),
            ring_bufs(half, CW),
            ring_bufs(RY, 5 * DH),
            V((RY, 5 * DH), BF16),
            V((2, nz, RZ // 2, 5 * DH), BF16),
            pair_bufs(),
            pair_bufs(),
            pair_bufs(),
            pltpu.SemaphoreType.DMA((11,)),
            pltpu.SemaphoreType.DMA((MAX_COPIES,)),
            pltpu.SemaphoreType.DMA((MAX_COPIES,)),
        ],
        compiler_params=pltpu.CompilerParams(
            collective_id=0, has_side_effects=True, vmem_limit_bytes=60 * 1024 * 1024
        ),
    )(
        inputs,
        proj_weight,
        out_weight,
        cotangent,
        block_history,
        event_mask.reshape(nblk, BLK),
    )
    return pl.pallas_call(
        hand_on,
        out_shape=out_shape,
        in_specs=[vmem] * 4,
        out_specs=(vmem,) * 4,
    )(*results)


def solution(mesh):
    nx = mesh.shape["head"]
    chips = mesh.shape["seq"] // 2
    nz = 8 if chips % 32 == 0 else 2
    ny = chips // nz
    return jax.shard_map(
        functools.partial(body, nx, ny, nz),
        mesh=mesh,
        in_specs=(
            P("seq", None),
            P(None, "head"),
            P(None, "head"),
            P("seq", None),
            P("seq"),
            P("seq"),
        ),
        out_specs=(P("seq", "head"), P("seq", "head"), P("seq", "head"), P("seq", "head")),
        check_vma=False,
    )
```

```python
import functools

import jax
import jax.numpy as jnp
from jax import lax
from jax.experimental import pallas as pl
from jax.experimental.pallas import tpu as pltpu
from jax.sharding import PartitionSpec as P

MESH = pl.DeviceIdType.MESH
DH = 128
BLK = 128
TILE = 256
F32 = jnp.float32
BF16 = jnp.bfloat16
NT = (((1,), (1,)), ((), ()))
MAX_COPIES = 128


def dot_nt(a, b):
    return lax.dot_general(a, b, NT, preferred_element_type=F32)


def dot_nn(a, b):
    return jnp.dot(a, b, preferred_element_type=F32)


def silu_parts(u, mask):
    t = jnp.tanh(u)
    p = 1.0 + t
    if mask is not None:
        p = p * mask
    w = u * p
    return w, p + w * (1.0 - t)


def layer_kernel(
    nx,
    ny,
    nz,
    token_total,
    inp,
    wp_hbm,
    wo_hbm,
    cot,
    history,
    events,
    lo_ref,
    gi_ref,
    gp_ref,
    go_ref,
    wo,
    wpp,
    xs,
    cs,
    xt,
    mxt,
    metas,
    ids,
    mk,
    mcol,
    slope,
    gate,
    kv,
    qh,
    dah,
    attn,
    gm,
    stat,
    mx,
    m2,
    gpre,
    g2,
    dq,
    dk,
    dv,
    lo_bufs,
    gi_bufs,
    w_bufs,
    w_s2,
    w_r2,
    q_slopes,
    k_weights,
    k_slopes,
    lsem,
    ssem,
    rsem,
):
    s = lax.axis_index("seq")
    x = lax.axis_index("head")
    r = lax.rem(s, 2)
    o = 1 - r
    c = s // 2
    nc = ny * nz
    z = lax.rem(c, nz)
    y = c // nz
    half = inp.shape[0]
    T = 2 * half
    D = inp.shape[1]
    CW = D // nx
    RY = D // ny
    RZ = RY // nz
    RC = RZ // 2
    nblk = T // BLK
    ntile = T // TILE
    scale = DH ** (-0.5)
    grad_scale = token_total ** (-0.5)

    own0 = pl.multiple_of(r * half, half)
    oth0 = pl.multiple_of(o * half, half)
    own_rows = pl.ds(own0, half)
    oth_rows = pl.ds(oth0, half)
    head_cols = pl.ds(pl.multiple_of(r * 4 * DH, 4 * DH), 4 * DH)
    gq_cols = pl.ds(pl.multiple_of(r * 4 * DH, 2 * DH), 2 * DH)
    kv_cols = pl.ds(pl.multiple_of(r * 4 * DH + 2 * DH, 2 * DH), 2 * DH)
    head_dh = pl.ds(pl.multiple_of(r * DH, DH), DH)

    def load_group(head, first, sems):
        copies = []
        for i in (first, first + 1):
            src = pl.ds(pl.multiple_of(head * 4 * DH + (0, 2, 1, 3)[i] * DH, DH), DH)
            dst = pl.ds(pl.multiple_of(head * 4 * DH + i * DH, DH), DH)
            copies.append(
                pltpu.make_async_copy(wp_hbm.at[:, src], wpp.at[:, dst], lsem.at[sems + i - first])
            )
        return copies

    load_x = pltpu.make_async_copy(inp, xs.at[own_rows], lsem.at[0])
    load_c = pltpu.make_async_copy(cot, cs.at[own_rows], lsem.at[1])
    load_wo = pltpu.make_async_copy(wo_hbm, wo, lsem.at[2])
    load_kv = load_group(r, 2, 3)
    load_gq = load_group(r, 0, 5)
    load_rest = load_group(o, 0, 7) + load_group(o, 2, 9)
    for copy in [load_x] + load_kv + load_gq + [load_c, load_wo] + load_rest:
        copy.start()

    def at_chip(chip):
        return (chip * 2 + r, x)

    chip_next = [lax.rem(c + d, nc) for d in (1, 2)]
    chip_prev = [lax.rem(c + nc - d, nc) for d in (1, 2)]
    partner = (c * 2 + o, x)

    def at_x(dx):
        return (s, lax.rem(x + nx + dx, nx))

    def at_y(dy):
        return at_chip(lax.rem(y + ny + dy, ny) * nz + z)

    def at_z(dz, dr):
        chip = y * nz + lax.rem(z + dz, nz)
        return (chip * 2 + lax.rem(r + dr, 2), x)

    group = []
    for dx in range(nx):
        for dr in range(2):
            if dx or dr:
                group.append((c * 2 + lax.rem(r + dr, 2), lax.rem(x + dx, nx)))
    peers = list(group)
    peers += [at_chip(k) for k in chip_next + chip_prev]
    peers += [at_y(d) for d in ((1, -1) if ny > 2 else (1,))]
    peers += [at_z(d, e) for d in range(1, nz) for e in range(2)]

    barrier = pltpu.get_barrier_semaphore()
    for peer in peers:
        pl.semaphore_signal(barrier, inc=1, device_id=peer, device_id_type=MESH)

    sent = []

    def push(src, dst, device):
        i = len(sent)
        copy = pltpu.make_async_remote_copy(
            src_ref=src,
            dst_ref=dst,
            send_sem=ssem.at[i],
            recv_sem=rsem.at[i],
            device_id=device,
            device_id_type=MESH,
        )
        copy.start()
        sent.append(copy)
        return copy

    def mask_columns(block_meta, row0):
        for b in range(nblk // 2):
            row = block_meta[4 + b : 5 + b, :].astype(F32)
            mcol[pl.ds(row0 + b * BLK, BLK), :] = jnp.broadcast_to(row, (BLK, BLK)).T

    def project_kv(row0):
        def step(t, carry):
            rows = pl.ds(pl.multiple_of(row0 + t * TILE, TILE), TILE)
            u = dot_nn(xs[rows, :], wpp[:, kv_cols]) * 0.5
            slope[rows, 2 * DH :] = u
            act = u * (1.0 + jnp.tanh(u))
            kv[0, rows, DH:] = act[:, :DH].astype(BF16)
            kv[0, rows, :DH] = (act[:, DH:] * mcol[rows, :]).astype(BF16)
            return carry

        lax.fori_loop(0, half // TILE, step, 0)

    def project_gq(row0):
        def step(t, carry):
            rows = pl.ds(pl.multiple_of(row0 + t * TILE, TILE), TILE)
            u = dot_nn(xs[rows, :], wpp[:, gq_cols]) * 0.5
            slope[rows, : 2 * DH] = u
            u = u[:, DH:]
            qh[0, rows, :] = (u * (1.0 + jnp.tanh(u)) * mcol[rows, :]).astype(BF16)
            return carry

        lax.fori_loop(0, half // TILE, step, 0)

    def gates_and_slopes(t, carry):
        rows = pl.ds(pl.multiple_of(t * BLK, BLK), BLK)
        act, slope2 = silu_parts(slope[rows, :], None)
        gate[rows, :] = act[:, :DH].astype(BF16)
        slope[rows, :] = 0.5 * slope2
        return carry

    own_meta = jnp.concatenate(
        [jnp.full((1, BLK), history[b], jnp.int32) for b in range(nblk // 2)] + [events[...]],
        axis=0,
    )
    metas[r] = own_meta
    mask_columns(own_meta, own0)
    load_x.wait()
    for copy in load_kv:
        copy.wait()
    project_kv(own0)

    pl.semaphore_wait(barrier, len(peers))
    kv_a = push(kv.at[0, own_rows], kv.at[1, own_rows], at_chip(chip_next[0]))
    swap_x = push(xs.at[own_rows], xs.at[own_rows], partner)
    swap_meta = push(metas.at[r], metas.at[r], partner)
    for copy in load_gq:
        copy.wait()
    project_gq(own0)
    q_a = push(qh.at[0, own_rows], qh.at[1, own_rows], at_chip(chip_prev[0]))
    load_c.wait()
    swap_c = push(cs.at[own_rows], cs.at[own_rows], partner)

    def turn(b, carry):
        rows = pl.ds(pl.multiple_of(b * BLK, BLK), BLK)
        xt[:, rows] = xs[rows, :].T
        return carry

    lax.fori_loop(r * (nblk // 2), (r + 1) * (nblk // 2), gates_and_slopes, 0)
    lax.fori_loop(r * (nblk // 2), (r + 1) * (nblk // 2), turn, 0)
    swap_meta.wait_recv()
    mask_columns(metas[o], oth0)
    swap_x.wait_recv()
    project_kv(oth0)
    kv_b = push(kv.at[0, oth_rows], kv.at[1, oth_rows], at_chip(chip_next[0]))
    project_gq(oth0)
    q_b = push(qh.at[0, oth_rows], qh.at[1, oth_rows], at_chip(chip_prev[0]))

    ids[0] = jnp.concatenate([metas[0][:4], metas[1][:4]], axis=0)
    id_copies = [
        push(ids.at[0], ids.at[1], at_chip(chip_next[0])),
        push(ids.at[0], ids.at[2], at_chip(chip_next[1])),
        push(ids.at[0], ids.at[3], at_chip(chip_prev[0])),
        push(ids.at[0], ids.at[4], at_chip(chip_prev[1])),
    ]

    def block_masks(slot):
        own = ids[0]
        other = ids[slot]
        for k in range(nblk):
            same = jnp.broadcast_to(other[k : k + 1, :], own.shape) == own
            mk[slot, :, k * BLK : (k + 1) * BLK] = jnp.where(same, 1.0, 0.0)

    def tile_rows(t):
        return pl.ds(t * TILE if isinstance(t, int) else pl.multiple_of(t * TILE, TILE), TILE)

    def tile_mask(slot, t, first, last):
        cols = slice(first * TILE, last * TILE)
        n = (last - first) * TILE
        return jnp.concatenate(
            [
                jnp.broadcast_to(
                    mk[slot, pl.ds((TILE // BLK) * t + i, 1), cols].astype(BF16), (BLK, n)
                )
                for i in range(TILE // BLK)
            ],
            axis=0,
        )

    def triangle(lower):
        row = lax.broadcasted_iota(jnp.int32, (TILE, TILE), 0)
        col = lax.broadcasted_iota(jnp.int32, (TILE, TILE), 1)
        return jnp.where(col <= row if lower else row <= col, 1.0, 0.0).astype(BF16)

    def query_mask(slot, t, first, last):
        mask = tile_mask(slot, t, first, last)
        if slot == 0:
            n = mask.shape[1] - TILE
            corner = mask[:, n:] * triangle(True)
            mask = jnp.concatenate([mask[:, :n], corner], axis=1) if n else corner
        return mask

    def key_mask(slot, t, first, last):
        mask = tile_mask(slot, t, first, last)
        if slot == 0:
            n = mask.shape[1] - TILE
            corner = mask[:, :TILE] * triangle(False)
            mask = jnp.concatenate([corner, mask[:, TILE:]], axis=1) if n else corner
        return mask

    def put(ref, rows, part, begin):
        ref[rows, :] = part if begin else ref[rows, :] + part

    def over_tiles(step, spans, tiles=range(ntile)):
        if spans is None:
            def body(t, carry):
                step(t, 0, ntile)
                return carry

            lax.fori_loop(0, ntile, body, 0)
        else:
            for t in tiles:
                step(t, *spans(t))

    def upto(t):
        return 0, t + 1

    def onward(t):
        return t, ntile

    def kept(bufs, j, shifted, rows, first, last):
        shift = 1 if j == shifted else 0
        cols = slice((first + shift) * TILE, (last + shift) * TILE)
        return bufs[j % 2].at[rows, cols]

    def attend(slot, spans, tiles=range(ntile)):
        def step(t, first, last):
            rows = tile_rows(t)
            cols = slice(first * TILE, last * TILE)
            u = (dot_nt(qh[0, rows, :], kv[slot, cols, :DH]) * (0.5 * scale)).astype(BF16)
            w, slope2 = silu_parts(u, query_mask(slot, t, first, last))
            put(attn, rows, dot_nn(w, kv[slot, cols, DH:]), slot == 0)
            kept(q_slopes, slot, 2, rows, first, last)[...] = slope2

        over_tiles(step, spans, tiles)

    def key_parts(j, spans):
        slot = 0 if j == 0 else 2 + j

        def step(t, first, last):
            rows = tile_rows(t)
            cols = slice(first * TILE, last * TILE)
            u = (dot_nt(kv[0, rows, :DH], qh[j, cols, :]) * (0.5 * scale)).astype(BF16)
            w, slope2 = silu_parts(u, key_mask(slot, t, first, last))
            kept(k_weights, j, 0, rows, first, last)[...] = w
            kept(k_slopes, j, 0, rows, first, last)[...] = slope2

        over_tiles(step, spans)

    block_masks(0)
    attend(0, upto)

    load_wo.wait()
    for copy in load_rest:
        copy.wait()
    swap_c.wait_recv()

    def grad_mix(t, carry):
        rows = tile_rows(t)
        gm[rows, :] = dot_nn(cs[rows, :], wo[:, head_dh])
        return carry

    def hop(src, dst, start, size, device):
        rows = pl.ds(start, size)
        i = len(sent)
        copy = pltpu.make_async_remote_copy(
            src_ref=src.at[rows],
            dst_ref=dst.at[rows],
            send_sem=ssem.at[i],
            recv_sem=rsem.at[i],
            device_id=device,
            device_id_type=MESH,
        )
        sent.append(copy)
        return copy

    kv_lo = hop(kv.at[1], kv.at[2], BLK, half - BLK, at_chip(chip_next[0]))
    kv_hi = hop(kv.at[1], kv.at[2], half, half, at_chip(chip_next[0]))
    q_lo = hop(qh.at[1], qh.at[2], 0, half, at_chip(chip_prev[0]))
    q_hi = hop(qh.at[1], qh.at[2], half, half - BLK, at_chip(chip_prev[0]))
    kv[2, :BLK, :] = jnp.zeros((BLK, 2 * DH), BF16)
    qh[2, T - BLK :, :] = jnp.zeros((BLK, DH), BF16)
    dah[2, T - BLK :, :] = jnp.zeros((BLK, DH), BF16)

    def start_one(first, second):
        pl.when(r == 0)(first.start)
        pl.when(r == 1)(second.start)

    kv_a.wait_recv()
    start_one(kv_lo, kv_hi)
    q_a.wait_recv()
    start_one(q_lo, q_hi)

    lax.fori_loop(0, ntile, grad_mix, 0)
    lax.fori_loop(o * (nblk // 2), (o + 1) * (nblk // 2), gates_and_slopes, 0)
    key_parts(0, onward)

    kv_b.wait_recv()
    start_one(kv_hi, kv_lo)
    q_b.wait_recv()
    start_one(q_hi, q_lo)
    for copy in id_copies:
        copy.wait_recv()
    for slot in range(1, 5):
        block_masks(slot)
    attend(1, None)

    lax.fori_loop(o * (nblk // 2), (o + 1) * (nblk // 2), turn, 0)
    key_parts(1, None)
    kv_lo.wait_recv()
    kv_hi.wait_recv()

    lane = lax.broadcasted_iota(jnp.int32, (BLK, BLK), 1)
    quarter = half // 2

    def send_sums(h):
        for b in range(quarter // BLK):
            packed = []
            for e in range(2):
                rows = pl.ds(h * half + e * quarter + b * BLK, BLK)
                a = attn[rows, :]
                gn = gm[rows, :] * gate[rows, :].astype(F32)
                sums = [a, a * a, gn, gn * a]
                column = jnp.zeros((BLK, BLK), F32)
                for i, term in enumerate(sums):
                    total = jnp.sum(term, axis=1, keepdims=True)
                    column = jnp.where(lane == 4 * e + i, total, column)
                packed.append(column)
            stat[h, 0, :, b * BLK : (b + 1) * BLK] = (packed[0] + packed[1]).T[:8, :]
        return [
            push(stat.at[h, 0], stat.at[h, i + 1], device) for i, device in enumerate(group)
        ]

    def normalise(h, copies):
        for copy in copies:
            copy.wait_recv()
        total = stat[h, 0]
        for i in range(len(group)):
            total = total + stat[h, i + 1]
        derived = []
        for e in range(2):
            s1, s2, s3, s4 = [total[4 * e + i : 4 * e + i + 1, :] for i in range(4)]
            mean = s1 / D
            inv = lax.rsqrt(s2 / D - mean * mean + 1e-05)
            derived += [mean, inv, s3 / D, (s4 - mean * s3) * inv / D]
        derived = jnp.concatenate(derived, axis=0)
        for b in range(quarter // BLK):
            columns = jnp.concatenate(
                [derived[:, b * BLK : (b + 1) * BLK], jnp.zeros((BLK - 8, BLK), F32)], axis=0
            ).T
            for e in range(2):
                rows = pl.ds(h * half + e * quarter + b * BLK, BLK)
                mean, inv, mean_grad, mean_cross = [
                    columns[:, 4 * e + i : 4 * e + i + 1] for i in range(4)
                ]
                g = gate[rows, :].astype(F32)
                grad_mixed = gm[rows, :]
                normed = (attn[rows, :] - mean) * inv
                dah[0, rows, :] = (
                    (grad_mixed * g - mean_grad - normed * mean_cross) * inv
                ).astype(BF16)
                mx[rows, :] = (normed * g).astype(BF16)
                gpre[rows, :DH] = (grad_mixed * normed * slope[rows, :DH]).astype(BF16)
        rows = pl.ds(h * half, half)
        return push(dah.at[0, rows], dah.at[1, rows], at_chip(chip_prev[0]))

    low, high = range(ntile // 2), range(ntile // 2, ntile)
    attend(2, onward, tiles=low)
    low_sums = send_sums(0)
    attend(2, onward, tiles=high)
    high_sums = send_sums(1)
    q_lo.wait_recv()
    q_hi.wait_recv()
    key_parts(2, upto)
    da_early = normalise(0, low_sums)
    da_late = normalise(1, high_sums)

    swap_mx = push(mx.at[oth_rows], m2.at[:, head_dh], partner)
    m2[:, head_dh] = mx[own_rows, :]

    def query_grads(slot, spans):
        def step(t, first, last):
            rows = tile_rows(t)
            cols = slice(first * TILE, last * TILE)
            gw = dot_nt(dah[0, rows, :], kv[slot, cols, DH:]).astype(BF16)
            ds = gw * kept(q_slopes, slot, 2, rows, first, last)[...]
            put(dq, rows, dot_nn(ds, kv[slot, cols, :DH]), slot == 0)

        over_tiles(step, spans)

    def key_grads(j, spans):
        def step(t, first, last):
            rows = tile_rows(t)
            cols = slice(first * TILE, last * TILE)
            gw = dot_nt(kv[0, rows, DH:], dah[j, cols, :]).astype(BF16)
            ds = gw * kept(k_slopes, j, 0, rows, first, last)[...]
            w = kept(k_weights, j, 0, rows, first, last)[...]
            put(dv, rows, dot_nn(w, dah[j, cols, :]), j == 0)
            put(dk, rows, dot_nn(ds, qh[j, cols, :]), j == 0)

        over_tiles(step, spans)

    def ring_far(n, device, term, bufs, cols):
        send, far, near, last, own = bufs
        h = far.shape[0] // 2
        early, late = pl.ds(0, h), pl.ds(h, h)
        if n != 4:
            return []
        send[0, :, cols] = term(2).astype(BF16)
        return [
            push(send.at[0, early, cols], far.at[early, cols], device(1)),
            push(send.at[0, late, cols], far.at[late, cols], device(-1)),
        ]

    def ring_near(n, device, term, bufs, cols):
        send, far, near, last, own = bufs
        h = far.shape[0] // 2
        early, late = pl.ds(0, h), pl.ds(h, h)
        part = term(1)
        near[0, :, cols] = part[:h, :]
        send[1, late, cols] = part[h:, :].astype(BF16)
        copies = [push(send.at[1, late, cols], last.at[0, late, cols], device(1))]
        if n == 4:
            part = term(3)
            near[1, :, cols] = part[h:, :]
            send[2, early, cols] = part[:h, :].astype(BF16)
            copies.append(push(send.at[2, early, cols], last.at[1, early, cols], device(-1)))
        return copies

    def ring_own(term, bufs, cols):
        bufs[4][:, cols] = term(0)

    def ring_first(n, device, term, bufs, cols):
        copies = ring_far(n, device, term, bufs, cols)
        copies += ring_near(n, device, term, bufs, cols)
        ring_own(term, bufs, cols)
        return copies

    def ring_second(n, device, bufs, cols, copies):
        send, far, near, last, own = bufs
        h = far.shape[0] // 2
        early, late = pl.ds(0, h), pl.ds(h, h)
        out = copies[2:] if n == 4 else copies
        part = near[0, :, cols]
        if n == 4:
            copies[0].wait_recv()
            part = part + far[early, cols].astype(F32)
        send[1, early, cols] = part.astype(BF16)
        out.append(push(send.at[1, early, cols], last.at[0, early, cols], device(1)))
        if n == 4:
            copies[1].wait_recv()
            part = near[1, :, cols] + far[late, cols].astype(F32)
            send[2, late, cols] = part.astype(BF16)
            out.append(push(send.at[2, late, cols], last.at[1, late, cols], device(-1)))
        return out

    def ring_total(bufs, cols, copies):
        send, far, near, last, own = bufs
        for copy in copies:
            copy.wait_recv()
        part = own[:, cols]
        for i in range(len(copies) // 2):
            part = part + last[i, :, cols].astype(F32)
        return part

    def weight_term(lhs_t, rhs):
        def term(d):
            at = pl.multiple_of(lax.rem(y + d, ny) * RY, RY)
            return dot_nn(lhs_t[pl.ds(at, RY), :], rhs)

        return term

    def model_term(rows_ref, weight):
        def term(d):
            at = pl.multiple_of(lax.rem(x + d, nx) * CW, CW)
            return dot_nt(rows_ref[...], weight[pl.ds(at, CW), :])

        return term

    def over_z(cols, copies):
        part = ring_total(w_bufs, cols, copies)
        w_bufs[4][:, cols] = part
        w_s2[:, cols] = part.astype(BF16)
        later = []
        for dz in range(nz):
            for dr in range(2):
                if dz or dr:
                    side = lax.rem(r + dr, 2)
                    at = pl.multiple_of(lax.rem(z + dz, nz) * RZ + side * RC, RC)
                    later.append(
                        push(
                            w_s2.at[pl.ds(at, RC), cols],
                            w_r2.at[dr, dz, :, cols],
                            at_z(dz, dr),
                        )
                    )
        return later

    every = pl.ds(0, CW)
    early_cols, late_cols = pl.ds(0, 3 * DH), pl.ds(3 * DH, 2 * DH)

    query_grads(0, upto)
    swap_mx.wait_recv()
    lo_first = ring_first(nx, at_x, model_term(m2, wo), lo_bufs, every)
    da_early.wait_recv()
    rows = pl.ds(0, half)
    da_fa = push(dah.at[1, rows], dah.at[2, rows], at_chip(chip_prev[0]))
    query_grads(1, None)
    da_late.wait_recv()
    rows = pl.ds(half, half - BLK)
    da_fb = push(dah.at[1, rows], dah.at[2, rows], at_chip(chip_prev[0]))
    lo_second = ring_second(nx, at_x, lo_bufs, every, lo_first)
    query_grads(2, onward)
    gpre[:, DH : 2 * DH] = (
        dq[...] * mcol[...] * (0.5 * scale) * slope[:, DH : 2 * DH]
    ).astype(BF16)
    early = pl.ds(pl.multiple_of(r * 4 * DH, 4 * DH), 2 * DH)
    late = pl.ds(pl.multiple_of(r * 4 * DH + 2 * DH, 2 * DH), 2 * DH)
    swap_early = push(gpre.at[oth_rows, : 2 * DH], g2.at[:, early], partner)
    for b in range(nblk):
        mxt[:, b * BLK : (b + 1) * BLK] = mx[b * BLK : (b + 1) * BLK, :].T

    def out_term(d):
        at = pl.multiple_of(lax.rem(y + d, ny) * RY, RY)
        return dot_nn(mxt[...], cs[:, pl.ds(at, RY)]).T

    query_term = weight_term(xt, gpre[:, : 2 * DH])

    def early_term(d):
        return jnp.concatenate([out_term(d), query_term(d)], axis=1)

    early_first = ring_first(ny, at_y, early_term, w_bufs, early_cols)
    key_grads(0, onward)
    early_second = ring_second(ny, at_y, w_bufs, early_cols, early_first)
    key_grads(1, None)
    early_z = over_z(early_cols, early_second)
    da_fa.wait_recv()
    da_fb.wait_recv()
    key_grads(2, upto)
    def late_grads(rows):
        gpre[rows, 2 * DH : 3 * DH] = (dv[rows, :] * slope[rows, 2 * DH : 3 * DH]).astype(BF16)
        gpre[rows, 3 * DH :] = (
            dk[rows, :] * mcol[rows, :] * (0.5 * scale) * slope[rows, 3 * DH :]
        ).astype(BF16)

    late_grads(oth_rows)
    settled = len(sent)
    swap_late = push(gpre.at[oth_rows, 2 * DH :], g2.at[:, late], partner)
    late_grads(own_rows)
    g2[:, head_cols] = gpre[own_rows, :]
    late_term = weight_term(xt, gpre[:, 2 * DH :])
    gi_term = model_term(g2, wpp)
    late_first = ring_far(ny, at_y, late_term, w_bufs, late_cols)
    swap_early.wait_recv()
    swap_late.wait_recv()
    gi_first = ring_far(nx, at_x, gi_term, gi_bufs, every)
    late_first += ring_near(ny, at_y, late_term, w_bufs, late_cols)
    gi_first += ring_near(nx, at_x, gi_term, gi_bufs, every)
    ring_own(late_term, w_bufs, late_cols)
    late_second = ring_second(ny, at_y, w_bufs, late_cols, late_first)
    gi_second = ring_second(nx, at_x, gi_bufs, every, gi_first)
    ring_own(gi_term, gi_bufs, every)
    late_z = over_z(late_cols, late_second)

    model_cols = pl.ds(pl.multiple_of(x * CW, CW), CW)
    lo = ring_total(lo_bufs, every, lo_second)
    lo_ref[...] = (xs[own_rows, model_cols].astype(F32) + lo).astype(BF16)

    for copy in sent[:settled]:
        copy.wait_send()
    for copy in early_z + late_z:
        copy.wait_recv()
    own_part = w_bufs[4][pl.ds(pl.multiple_of(z * RZ + r * RC, RC), RC), :]
    for dr in range(2):
        part = own_part if dr == 0 else w_r2[1, 0].astype(F32)
        for dz in range(1, nz):
            part = part + w_r2[dr, dz].astype(F32)
        part = part * grad_scale
        side = lax.rem(r + dr, 2)
        go_ref[:, pl.ds(pl.multiple_of(side * DH, DH), DH)] = part[:, :DH]
        for p, i in enumerate((1, 3, 2, 4)):
            cols = pl.ds(pl.multiple_of(side * 4 * DH + p * DH, DH), DH)
            gp_ref[:, cols] = part[:, i * DH : (i + 1) * DH]

    gi = ring_total(gi_bufs, every, gi_second)
    gi_ref[...] = (cs[own_rows, model_cols].astype(F32) + gi).astype(BF16)

    for copy in sent[settled:]:
        copy.wait_send()


def hand_on(*refs):
    n = len(refs) // 2
    copies = [
        pltpu.make_async_copy(refs[i], refs[n + i], refs[2 * n].at[i]) for i in range(n)
    ]
    for copy in copies:
        copy.start()
    for copy in copies:
        copy.wait()


def body(nx, ny, nz, inputs, proj_weight, out_weight, cotangent, block_history, event_mask):
    half, D = inputs.shape
    T = 2 * half
    CW = D // nx
    RY = D // ny
    RZ = RY // nz
    nblk = half // BLK
    vmem = pl.BlockSpec(memory_space=pltpu.VMEM)
    hbm = pl.BlockSpec(memory_space=pltpu.HBM)
    V = pltpu.VMEM

    def ring_bufs(rows, cols):
        return (
            V((3, rows, cols), BF16),
            V((rows, cols), BF16),
            V((2, rows // 2, cols), F32),
            V((2, rows, cols), BF16),
            V((rows, cols), F32),
        )

    def pair_bufs():
        return V((T, T + TILE), BF16), V((T, T), BF16)

    out_shape = (
        jax.ShapeDtypeStruct((half, CW), BF16),
        jax.ShapeDtypeStruct((half, CW), BF16),
        jax.ShapeDtypeStruct((RZ // 2, 8 * DH), F32),
        jax.ShapeDtypeStruct((RZ // 2, 2 * DH), F32),
    )
    results = pl.pallas_call(
        functools.partial(layer_kernel, nx, ny, nz, half * 2 * ny * nz),
        out_shape=tuple(V(out.shape, out.dtype) for out in out_shape),
        in_specs=[hbm] * 4 + [pl.BlockSpec(memory_space=pltpu.SMEM), vmem],
        out_specs=(vmem,) * 4,
        scratch_shapes=[
            V((D, 2 * DH), BF16),
            V((D, 8 * DH), BF16),
            V((T, D), BF16),
            V((T, D), BF16),
            V((D, T), BF16),
            V((DH, T), BF16),
            V((2, 8, BLK), jnp.int32),
            V((5, 8, BLK), jnp.int32),
            V((5, 8, T), F32),
            V((T, DH), F32),
            V((T, 4 * DH), F32),
            V((T, DH), BF16),
            V((3, T, 2 * DH), BF16),
            V((3, T, DH), BF16),
            V((3, T, DH), BF16),
            V((T, DH), F32),
            V((T, DH), F32),
            V((2, 2 * nx, 8, half // 2), F32),
            V((T, DH), BF16),
            V((half, 2 * DH), BF16),
            V((T, 4 * DH), BF16),
            V((half, 8 * DH), BF16),
            V((T, DH), F32),
            V((T, DH), F32),
            V((T, DH), F32),
            ring_bufs(half, CW),
            ring_bufs(half, CW),
            ring_bufs(RY, 5 * DH),
            V((RY, 5 * DH), BF16),
            V((2, nz, RZ // 2, 5 * DH), BF16),
            pair_bufs(),
            pair_bufs(),
            pair_bufs(),
            pltpu.SemaphoreType.DMA((11,)),
            pltpu.SemaphoreType.DMA((MAX_COPIES,)),
            pltpu.SemaphoreType.DMA((MAX_COPIES,)),
        ],
        compiler_params=pltpu.CompilerParams(
            collective_id=0, has_side_effects=True, vmem_limit_bytes=56 * 1024 * 1024
        ),
    )(
        inputs,
        proj_weight,
        out_weight,
        cotangent,
        block_history,
        event_mask.reshape(nblk, BLK),
    )
    return pl.pallas_call(
        hand_on,
        out_shape=out_shape,
        in_specs=[vmem] * 4,
        out_specs=(hbm,) * 4,
        scratch_shapes=[pltpu.SemaphoreType.DMA((4,))],
    )(*results)


def solution(mesh):
    nx = mesh.shape["head"]
    chips = mesh.shape["seq"] // 2
    nz = 8 if chips % 32 == 0 else 2
    ny = chips // nz
    return jax.shard_map(
        functools.partial(body, nx, ny, nz),
        mesh=mesh,
        in_specs=(
            P("seq", None),
            P(None, "head"),
            P(None, "head"),
            P("seq", None),
            P("seq"),
            P("seq"),
        ),
        out_specs=(P("seq", "head"), P("seq", "head"), P("seq", "head"), P("seq", "head")),
        check_vma=False,
    )
```

```python
import functools

import jax
import jax.numpy as jnp
from jax import lax
from jax.experimental import pallas as pl
from jax.experimental.pallas import tpu as pltpu
from jax.sharding import PartitionSpec as P

MESH = pl.DeviceIdType.MESH
DH = 128
BLK = 128
TILE = 256
F32 = jnp.float32
BF16 = jnp.bfloat16
NT = (((1,), (1,)), ((), ()))
MAX_COPIES = 128


def dot_nt(a, b):
    return lax.dot_general(a, b, NT, preferred_element_type=F32)


def dot_nn(a, b):
    return jnp.dot(a, b, preferred_element_type=F32)


def silu_parts(u, mask):
    t = jnp.tanh(u)
    p = 1.0 + t
    if mask is not None:
        p = p * mask
    w = u * p
    return w, p + w * (1.0 - t)


def layer_kernel(
    nx,
    ny,
    nz,
    token_total,
    inp,
    wp_hbm,
    wo_hbm,
    cot,
    history,
    events,
    lo_ref,
    gi_ref,
    gp_ref,
    go_ref,
    wo,
    wpp,
    xs,
    cs,
    xt,
    mxt,
    metas,
    ids,
    mk,
    mcol,
    slope,
    gate,
    kv,
    qh,
    dah,
    attn,
    gm,
    stat,
    mx,
    m2,
    gpre,
    g2,
    dq,
    dk,
    dv,
    lo_bufs,
    gi_bufs,
    w_bufs,
    w_s2,
    w_r2,
    q_slopes,
    k_weights,
    k_slopes,
    lsem,
    ssem,
    rsem,
):
    s = lax.axis_index("seq")
    x = lax.axis_index("head")
    r = lax.rem(s, 2)
    o = 1 - r
    c = s // 2
    nc = ny * nz
    z = lax.rem(c, nz)
    y = c // nz
    half = inp.shape[0]
    T = 2 * half
    D = inp.shape[1]
    CW = D // nx
    RY = D // ny
    RZ = RY // nz
    RC = RZ // 2
    nblk = T // BLK
    ntile = T // TILE
    scale = DH ** (-0.5)
    grad_scale = token_total ** (-0.5)

    own0 = pl.multiple_of(r * half, half)
    oth0 = pl.multiple_of(o * half, half)
    own_rows = pl.ds(own0, half)
    oth_rows = pl.ds(oth0, half)
    head_cols = pl.ds(pl.multiple_of(r * 4 * DH, 4 * DH), 4 * DH)
    gq_cols = pl.ds(pl.multiple_of(r * 4 * DH, 2 * DH), 2 * DH)
    kv_cols = pl.ds(pl.multiple_of(r * 4 * DH + 2 * DH, 2 * DH), 2 * DH)
    head_dh = pl.ds(pl.multiple_of(r * DH, DH), DH)

    def load_group(head, first, sems):
        copies = []
        for i in (first, first + 1):
            src = pl.ds(pl.multiple_of(head * 4 * DH + (0, 2, 1, 3)[i] * DH, DH), DH)
            dst = pl.ds(pl.multiple_of(head * 4 * DH + i * DH, DH), DH)
            copies.append(
                pltpu.make_async_copy(wp_hbm.at[:, src], wpp.at[:, dst], lsem.at[sems + i - first])
            )
        return copies

    load_x = pltpu.make_async_copy(inp, xs.at[own_rows], lsem.at[0])
    load_c = pltpu.make_async_copy(cot, cs.at[own_rows], lsem.at[1])
    load_wo = pltpu.make_async_copy(wo_hbm, wo, lsem.at[2])
    load_kv = load_group(r, 2, 3)
    load_gq = load_group(r, 0, 5)
    load_rest = load_group(o, 0, 7) + load_group(o, 2, 9)
    for copy in [load_x] + load_kv + load_gq + [load_c, load_wo] + load_rest:
        copy.start()

    def at_chip(chip):
        return (chip * 2 + r, x)

    chip_next = [lax.rem(c + d, nc) for d in (1, 2)]
    chip_prev = [lax.rem(c + nc - d, nc) for d in (1, 2)]
    partner = (c * 2 + o, x)

    def at_x(dx):
        return (s, lax.rem(x + nx + dx, nx))

    def at_y(dy):
        return at_chip(lax.rem(y + ny + dy, ny) * nz + z)

    def at_z(dz, dr):
        chip = y * nz + lax.rem(z + dz, nz)
        return (chip * 2 + lax.rem(r + dr, 2), x)

    group = []
    for dx in range(nx):
        for dr in range(2):
            if dx or dr:
                group.append((c * 2 + lax.rem(r + dr, 2), lax.rem(x + dx, nx)))
    peers = list(group)
    peers += [at_chip(k) for k in chip_next + chip_prev]
    peers += [at_y(d) for d in ((1, -1) if ny > 2 else (1,))]
    peers += [at_z(d, e) for d in range(1, nz) for e in range(2)]

    barrier = pltpu.get_barrier_semaphore()
    for peer in peers:
        pl.semaphore_signal(barrier, inc=1, device_id=peer, device_id_type=MESH)

    sent = []

    def push(src, dst, device):
        i = len(sent)
        copy = pltpu.make_async_remote_copy(
            src_ref=src,
            dst_ref=dst,
            send_sem=ssem.at[i],
            recv_sem=rsem.at[i],
            device_id=device,
            device_id_type=MESH,
        )
        copy.start()
        sent.append(copy)
        return copy

    def mask_columns(block_meta, row0):
        for b in range(nblk // 2):
            row = block_meta[4 + b : 5 + b, :].astype(F32)
            mcol[pl.ds(row0 + b * BLK, BLK), :] = jnp.broadcast_to(row, (BLK, BLK)).T

    def project_kv(row0):
        def step(t, carry):
            rows = pl.ds(pl.multiple_of(row0 + t * TILE, TILE), TILE)
            u = dot_nn(xs[rows, :], wpp[:, kv_cols]) * 0.5
            slope[rows, 2 * DH :] = u
            act = u * (1.0 + jnp.tanh(u))
            kv[0, rows, DH:] = act[:, :DH].astype(BF16)
            kv[0, rows, :DH] = (act[:, DH:] * mcol[rows, :]).astype(BF16)
            return carry

        lax.fori_loop(0, half // TILE, step, 0)

    def project_gq(row0):
        def step(t, carry):
            rows = pl.ds(pl.multiple_of(row0 + t * TILE, TILE), TILE)
            u = dot_nn(xs[rows, :], wpp[:, gq_cols]) * 0.5
            slope[rows, : 2 * DH] = u
            u = u[:, DH:]
            qh[0, rows, :] = (u * (1.0 + jnp.tanh(u)) * mcol[rows, :]).astype(BF16)
            return carry

        lax.fori_loop(0, half // TILE, step, 0)

    def gates_and_slopes(t, carry):
        rows = pl.ds(pl.multiple_of(t * BLK, BLK), BLK)
        act, slope2 = silu_parts(slope[rows, :], None)
        gate[rows, :] = act[:, :DH].astype(BF16)
        slope[rows, :] = 0.5 * slope2
        return carry

    own_meta = jnp.concatenate(
        [jnp.full((1, BLK), history[b], jnp.int32) for b in range(nblk // 2)] + [events[...]],
        axis=0,
    )
    metas[r] = own_meta
    mask_columns(own_meta, own0)
    load_x.wait()
    for copy in load_kv:
        copy.wait()
    project_kv(own0)

    pl.semaphore_wait(barrier, len(peers))
    kv_a = push(kv.at[0, own_rows], kv.at[1, own_rows], at_chip(chip_next[0]))
    swap_x = push(xs.at[own_rows], xs.at[own_rows], partner)
    swap_meta = push(metas.at[r], metas.at[r], partner)
    for copy in load_gq:
        copy.wait()
    project_gq(own0)
    q_a = push(qh.at[0, own_rows], qh.at[1, own_rows], at_chip(chip_prev[0]))
    load_c.wait()
    swap_c = push(cs.at[own_rows], cs.at[own_rows], partner)

    def turn(b, carry):
        rows = pl.ds(pl.multiple_of(b * BLK, BLK), BLK)
        xt[:, rows] = xs[rows, :].T
        return carry

    lax.fori_loop(r * (nblk // 2), (r + 1) * (nblk // 2), gates_and_slopes, 0)
    lax.fori_loop(r * (nblk // 2), (r + 1) * (nblk // 2), turn, 0)
    swap_meta.wait_recv()
    mask_columns(metas[o], oth0)
    swap_x.wait_recv()
    project_kv(oth0)
    kv_b = push(kv.at[0, oth_rows], kv.at[1, oth_rows], at_chip(chip_next[0]))
    project_gq(oth0)
    q_b = push(qh.at[0, oth_rows], qh.at[1, oth_rows], at_chip(chip_prev[0]))

    ids[0] = jnp.concatenate([metas[0][:4], metas[1][:4]], axis=0)
    id_copies = [
        push(ids.at[0], ids.at[1], at_chip(chip_next[0])),
        push(ids.at[0], ids.at[2], at_chip(chip_next[1])),
        push(ids.at[0], ids.at[3], at_chip(chip_prev[0])),
        push(ids.at[0], ids.at[4], at_chip(chip_prev[1])),
    ]

    def block_masks(slot):
        own = ids[0]
        other = ids[slot]
        for k in range(nblk):
            same = jnp.broadcast_to(other[k : k + 1, :], own.shape) == own
            mk[slot, :, k * BLK : (k + 1) * BLK] = jnp.where(same, 1.0, 0.0)

    def tile_rows(t):
        return pl.ds(t * TILE if isinstance(t, int) else pl.multiple_of(t * TILE, TILE), TILE)

    def tile_mask(slot, t, first, last):
        cols = slice(first * TILE, last * TILE)
        n = (last - first) * TILE
        return jnp.concatenate(
            [
                jnp.broadcast_to(
                    mk[slot, pl.ds((TILE // BLK) * t + i, 1), cols].astype(BF16), (BLK, n)
                )
                for i in range(TILE // BLK)
            ],
            axis=0,
        )

    def triangle(lower):
        row = lax.broadcasted_iota(jnp.int32, (TILE, TILE), 0)
        col = lax.broadcasted_iota(jnp.int32, (TILE, TILE), 1)
        return jnp.where(col <= row if lower else row <= col, 1.0, 0.0).astype(BF16)

    def query_mask(slot, t, first, last):
        mask = tile_mask(slot, t, first, last)
        if slot == 0:
            n = mask.shape[1] - TILE
            corner = mask[:, n:] * triangle(True)
            mask = jnp.concatenate([mask[:, :n], corner], axis=1) if n else corner
        return mask

    def key_mask(slot, t, first, last):
        mask = tile_mask(slot, t, first, last)
        if slot == 0:
            n = mask.shape[1] - TILE
            corner = mask[:, :TILE] * triangle(False)
            mask = jnp.concatenate([corner, mask[:, TILE:]], axis=1) if n else corner
        return mask

    def put(ref, rows, part, begin):
        ref[rows, :] = part if begin else ref[rows, :] + part

    def over_tiles(step, spans, tiles=range(ntile)):
        if spans is None:
            def body(t, carry):
                step(t, 0, ntile)
                return carry

            lax.fori_loop(0, ntile, body, 0)
        else:
            for t in tiles:
                step(t, *spans(t))

    def upto(t):
        return 0, t + 1

    def onward(t):
        return t, ntile

    def kept(bufs, j, shifted, rows, first, last):
        shift = 1 if j == shifted else 0
        cols = slice((first + shift) * TILE, (last + shift) * TILE)
        return bufs[j % 2].at[rows, cols]

    def attend(slot, spans, tiles=range(ntile)):
        def step(t, first, last):
            rows = tile_rows(t)
            cols = slice(first * TILE, last * TILE)
            u = (dot_nt(qh[0, rows, :], kv[slot, cols, :DH]) * (0.5 * scale)).astype(BF16)
            w, slope2 = silu_parts(u, query_mask(slot, t, first, last))
            put(attn, rows, dot_nn(w, kv[slot, cols, DH:]), slot == 0)
            kept(q_slopes, slot, 2, rows, first, last)[...] = slope2

        over_tiles(step, spans, tiles)

    def key_parts(j, spans):
        slot = 0 if j == 0 else 2 + j

        def step(t, first, last):
            rows = tile_rows(t)
            cols = slice(first * TILE, last * TILE)
            u = (dot_nt(kv[0, rows, :DH], qh[j, cols, :]) * (0.5 * scale)).astype(BF16)
            w, slope2 = silu_parts(u, key_mask(slot, t, first, last))
            kept(k_weights, j, 0, rows, first, last)[...] = w
            kept(k_slopes, j, 0, rows, first, last)[...] = slope2

        over_tiles(step, spans)

    block_masks(0)
    attend(0, upto)

    load_wo.wait()
    for copy in load_rest:
        copy.wait()
    swap_c.wait_recv()

    def grad_mix(t, carry):
        rows = tile_rows(t)
        gm[rows, :] = dot_nn(cs[rows, :], wo[:, head_dh])
        return carry

    def hop(src, dst, start, size, device):
        rows = pl.ds(start, size)
        i = len(sent)
        copy = pltpu.make_async_remote_copy(
            src_ref=src.at[rows],
            dst_ref=dst.at[rows],
            send_sem=ssem.at[i],
            recv_sem=rsem.at[i],
            device_id=device,
            device_id_type=MESH,
        )
        sent.append(copy)
        return copy

    kv_lo = hop(kv.at[1], kv.at[2], BLK, half - BLK, at_chip(chip_next[0]))
    kv_hi = hop(kv.at[1], kv.at[2], half, half, at_chip(chip_next[0]))
    q_lo = hop(qh.at[1], qh.at[2], 0, half, at_chip(chip_prev[0]))
    q_hi = hop(qh.at[1], qh.at[2], half, half - BLK, at_chip(chip_prev[0]))
    kv[2, :BLK, :] = jnp.zeros((BLK, 2 * DH), BF16)
    qh[2, T - BLK :, :] = jnp.zeros((BLK, DH), BF16)
    dah[2, T - BLK :, :] = jnp.zeros((BLK, DH), BF16)

    def start_one(first, second):
        pl.when(r == 0)(first.start)
        pl.when(r == 1)(second.start)

    kv_a.wait_recv()
    pl.when(r == 1)(kv_hi.start)
    q_a.wait_recv()
    start_one(q_lo, q_hi)

    lax.fori_loop(0, ntile, grad_mix, 0)
    lax.fori_loop(o * (nblk // 2), (o + 1) * (nblk // 2), gates_and_slopes, 0)
    key_parts(0, onward)

    kv_b.wait_recv()
    pl.when(r == 0)(kv_hi.start)
    kv_lo.start()
    q_b.wait_recv()
    start_one(q_hi, q_lo)
    for copy in id_copies:
        copy.wait_recv()
    for slot in range(1, 5):
        block_masks(slot)
    attend(1, None)

    lax.fori_loop(o * (nblk // 2), (o + 1) * (nblk // 2), turn, 0)
    key_parts(1, None)
    kv_hi.wait_recv()

    lane = lax.broadcasted_iota(jnp.int32, (BLK, BLK), 1)
    quarter = half // 2

    def send_sums(h):
        for b in range(quarter // BLK):
            packed = []
            for e in range(2):
                rows = pl.ds(h * half + e * quarter + b * BLK, BLK)
                a = attn[rows, :]
                gn = gm[rows, :] * gate[rows, :].astype(F32)
                sums = [a, a * a, gn, gn * a]
                column = jnp.zeros((BLK, BLK), F32)
                for i, term in enumerate(sums):
                    total = jnp.sum(term, axis=1, keepdims=True)
                    column = jnp.where(lane == 4 * e + i, total, column)
                packed.append(column)
            stat[h, 0, :, b * BLK : (b + 1) * BLK] = (packed[0] + packed[1]).T[:8, :]
        return [
            push(stat.at[h, 0], stat.at[h, i + 1], device) for i, device in enumerate(group)
        ]

    def normalise(h, copies):
        for copy in copies:
            copy.wait_recv()
        total = stat[h, 0]
        for i in range(len(group)):
            total = total + stat[h, i + 1]
        derived = []
        for e in range(2):
            s1, s2, s3, s4 = [total[4 * e + i : 4 * e + i + 1, :] for i in range(4)]
            mean = s1 / D
            inv = lax.rsqrt(s2 / D - mean * mean + 1e-05)
            derived += [mean, inv, s3 / D, (s4 - mean * s3) * inv / D]
        derived = jnp.concatenate(derived, axis=0)
        for b in range(quarter // BLK):
            columns = jnp.concatenate(
                [derived[:, b * BLK : (b + 1) * BLK], jnp.zeros((BLK - 8, BLK), F32)], axis=0
            ).T
            for e in range(2):
                rows = pl.ds(h * half + e * quarter + b * BLK, BLK)
                mean, inv, mean_grad, mean_cross = [
                    columns[:, 4 * e + i : 4 * e + i + 1] for i in range(4)
                ]
                g = gate[rows, :].astype(F32)
                grad_mixed = gm[rows, :]
                normed = (attn[rows, :] - mean) * inv
                dah[0, rows, :] = (
                    (grad_mixed * g - mean_grad - normed * mean_cross) * inv
                ).astype(BF16)
                mx[rows, :] = (normed * g).astype(BF16)
                gpre[rows, :DH] = (grad_mixed * normed * slope[rows, :DH]).astype(BF16)
        rows = pl.ds(h * half, half)
        return push(dah.at[0, rows], dah.at[1, rows], at_chip(chip_prev[0]))

    def query_grads(slot, spans, tiles):
        def step(t, first, last):
            rows = tile_rows(t)
            cols = slice(first * TILE, last * TILE)
            gw = dot_nt(dah[0, rows, :], kv[slot, cols, DH:]).astype(BF16)
            ds = gw * kept(q_slopes, slot, 2, rows, first, last)[...]
            put(dq, rows, dot_nn(ds, kv[slot, cols, :DH]), slot == 0)

        over_tiles(step, spans, tiles)

    def whole(t):
        return 0, ntile

    low, high = range(ntile // 2), range(ntile // 2, ntile)
    attend(2, onward, tiles=high)
    high_sums = send_sums(1)
    q_lo.wait_recv()
    q_hi.wait_recv()
    key_parts(2, upto)
    da_late = normalise(1, high_sums)
    query_grads(0, upto, high)
    query_grads(1, whole, high)
    kv_lo.wait_recv()
    attend(2, onward, tiles=low)
    low_sums = send_sums(0)
    query_grads(2, onward, high)
    da_late.wait_recv()
    rows = pl.ds(half, half - BLK)
    da_fb = push(dah.at[1, rows], dah.at[2, rows], at_chip(chip_prev[0]))
    da_early = normalise(0, low_sums)

    swap_mx = push(mx.at[oth_rows], m2.at[:, head_dh], partner)
    m2[:, head_dh] = mx[own_rows, :]

    def key_grads(j, spans):
        def step(t, first, last):
            rows = tile_rows(t)
            cols = slice(first * TILE, last * TILE)
            gw = dot_nt(kv[0, rows, DH:], dah[j, cols, :]).astype(BF16)
            ds = gw * kept(k_slopes, j, 0, rows, first, last)[...]
            w = kept(k_weights, j, 0, rows, first, last)[...]
            put(dv, rows, dot_nn(w, dah[j, cols, :]), j == 0)
            put(dk, rows, dot_nn(ds, qh[j, cols, :]), j == 0)

        over_tiles(step, spans)

    def ring_far(n, device, term, bufs, cols):
        send, far, near, last, own = bufs
        h = far.shape[0] // 2
        early, late = pl.ds(0, h), pl.ds(h, h)
        if n != 4:
            return []
        send[0, :, cols] = term(2).astype(BF16)
        return [
            push(send.at[0, early, cols], far.at[early, cols], device(1)),
            push(send.at[0, late, cols], far.at[late, cols], device(-1)),
        ]

    def ring_near(n, device, term, bufs, cols):
        send, far, near, last, own = bufs
        h = far.shape[0] // 2
        early, late = pl.ds(0, h), pl.ds(h, h)
        part = term(1)
        near[0, :, cols] = part[:h, :]
        send[1, late, cols] = part[h:, :].astype(BF16)
        copies = [push(send.at[1, late, cols], last.at[0, late, cols], device(1))]
        if n == 4:
            part = term(3)
            near[1, :, cols] = part[h:, :]
            send[2, early, cols] = part[:h, :].astype(BF16)
            copies.append(push(send.at[2, early, cols], last.at[1, early, cols], device(-1)))
        return copies

    def ring_own(term, bufs, cols):
        bufs[4][:, cols] = term(0)

    def ring_first(n, device, term, bufs, cols):
        copies = ring_far(n, device, term, bufs, cols)
        copies += ring_near(n, device, term, bufs, cols)
        ring_own(term, bufs, cols)
        return copies

    def ring_second(n, device, bufs, cols, copies):
        send, far, near, last, own = bufs
        h = far.shape[0] // 2
        early, late = pl.ds(0, h), pl.ds(h, h)
        out = copies[2:] if n == 4 else copies
        part = near[0, :, cols]
        if n == 4:
            copies[0].wait_recv()
            part = part + far[early, cols].astype(F32)
        send[1, early, cols] = part.astype(BF16)
        out.append(push(send.at[1, early, cols], last.at[0, early, cols], device(1)))
        if n == 4:
            copies[1].wait_recv()
            part = near[1, :, cols] + far[late, cols].astype(F32)
            send[2, late, cols] = part.astype(BF16)
            out.append(push(send.at[2, late, cols], last.at[1, late, cols], device(-1)))
        return out

    def ring_total(bufs, cols, copies):
        send, far, near, last, own = bufs
        for copy in copies:
            copy.wait_recv()
        part = own[:, cols]
        for i in range(len(copies) // 2):
            part = part + last[i, :, cols].astype(F32)
        return part

    def weight_term(lhs_t, rhs):
        def term(d):
            at = pl.multiple_of(lax.rem(y + d, ny) * RY, RY)
            return dot_nn(lhs_t[pl.ds(at, RY), :], rhs)

        return term

    def model_term(rows_ref, weight):
        def term(d):
            at = pl.multiple_of(lax.rem(x + d, nx) * CW, CW)
            return dot_nt(rows_ref[...], weight[pl.ds(at, CW), :])

        return term

    def over_z(cols, copies):
        part = ring_total(w_bufs, cols, copies)
        w_bufs[4][:, cols] = part
        w_s2[:, cols] = part.astype(BF16)
        later = []
        for dz in range(nz):
            for dr in range(2):
                if dz or dr:
                    side = lax.rem(r + dr, 2)
                    at = pl.multiple_of(lax.rem(z + dz, nz) * RZ + side * RC, RC)
                    later.append(
                        push(
                            w_s2.at[pl.ds(at, RC), cols],
                            w_r2.at[dr, dz, :, cols],
                            at_z(dz, dr),
                        )
                    )
        return later

    every = pl.ds(0, CW)
    early_cols, late_cols = pl.ds(0, 3 * DH), pl.ds(3 * DH, 2 * DH)

    query_grads(0, upto, low)
    swap_mx.wait_recv()
    lo_first = ring_first(nx, at_x, model_term(m2, wo), lo_bufs, every)
    da_early.wait_recv()
    rows = pl.ds(0, half)
    da_fa = push(dah.at[1, rows], dah.at[2, rows], at_chip(chip_prev[0]))
    query_grads(1, whole, low)
    lo_second = ring_second(nx, at_x, lo_bufs, every, lo_first)
    query_grads(2, onward, low)
    gpre[:, DH : 2 * DH] = (
        dq[...] * mcol[...] * (0.5 * scale) * slope[:, DH : 2 * DH]
    ).astype(BF16)
    early = pl.ds(pl.multiple_of(r * 4 * DH, 4 * DH), 2 * DH)
    late = pl.ds(pl.multiple_of(r * 4 * DH + 2 * DH, 2 * DH), 2 * DH)
    swap_early = push(gpre.at[oth_rows, : 2 * DH], g2.at[:, early], partner)
    for b in range(nblk):
        mxt[:, b * BLK : (b + 1) * BLK] = mx[b * BLK : (b + 1) * BLK, :].T

    def out_term(d):
        at = pl.multiple_of(lax.rem(y + d, ny) * RY, RY)
        return dot_nn(mxt[...], cs[:, pl.ds(at, RY)]).T

    query_term = weight_term(xt, gpre[:, : 2 * DH])

    def early_term(d):
        return jnp.concatenate([out_term(d), query_term(d)], axis=1)

    early_first = ring_first(ny, at_y, early_term, w_bufs, early_cols)
    key_grads(0, onward)
    early_second = ring_second(ny, at_y, w_bufs, early_cols, early_first)
    key_grads(1, None)
    early_z = over_z(early_cols, early_second)
    da_fa.wait_recv()
    da_fb.wait_recv()
    key_grads(2, upto)
    def late_grads(rows):
        gpre[rows, 2 * DH : 3 * DH] = (dv[rows, :] * slope[rows, 2 * DH : 3 * DH]).astype(BF16)
        gpre[rows, 3 * DH :] = (
            dk[rows, :] * mcol[rows, :] * (0.5 * scale) * slope[rows, 3 * DH :]
        ).astype(BF16)

    late_grads(oth_rows)
    settled = len(sent)
    swap_late = push(gpre.at[oth_rows, 2 * DH :], g2.at[:, late], partner)
    late_grads(own_rows)
    g2[:, head_cols] = gpre[own_rows, :]
    late_term = weight_term(xt, gpre[:, 2 * DH :])
    gi_term = model_term(g2, wpp)
    late_first = ring_far(ny, at_y, late_term, w_bufs, late_cols)
    swap_early.wait_recv()
    swap_late.wait_recv()
    gi_first = ring_far(nx, at_x, gi_term, gi_bufs, every)
    late_first += ring_near(ny, at_y, late_term, w_bufs, late_cols)
    gi_first += ring_near(nx, at_x, gi_term, gi_bufs, every)
    ring_own(late_term, w_bufs, late_cols)
    late_second = ring_second(ny, at_y, w_bufs, late_cols, late_first)
    gi_second = ring_second(nx, at_x, gi_bufs, every, gi_first)
    ring_own(gi_term, gi_bufs, every)
    late_z = over_z(late_cols, late_second)

    model_cols = pl.ds(pl.multiple_of(x * CW, CW), CW)
    lo = ring_total(lo_bufs, every, lo_second)
    lo_ref[...] = (xs[own_rows, model_cols].astype(F32) + lo).astype(BF16)

    for copy in sent[:settled]:
        copy.wait_send()
    for copy in early_z + late_z:
        copy.wait_recv()
    own_part = w_bufs[4][pl.ds(pl.multiple_of(z * RZ + r * RC, RC), RC), :]
    for dr in range(2):
        part = own_part if dr == 0 else w_r2[1, 0].astype(F32)
        for dz in range(1, nz):
            part = part + w_r2[dr, dz].astype(F32)
        part = part * grad_scale
        side = lax.rem(r + dr, 2)
        go_ref[:, pl.ds(pl.multiple_of(side * DH, DH), DH)] = part[:, :DH]
        for p, i in enumerate((1, 3, 2, 4)):
            cols = pl.ds(pl.multiple_of(side * 4 * DH + p * DH, DH), DH)
            gp_ref[:, cols] = part[:, i * DH : (i + 1) * DH]

    gi = ring_total(gi_bufs, every, gi_second)
    gi_ref[...] = (cs[own_rows, model_cols].astype(F32) + gi).astype(BF16)

    for copy in sent[settled:]:
        copy.wait_send()


def hand_on(*refs):
    n = len(refs) // 2
    for src, dst in zip(refs[:n], refs[n:]):
        dst[...] = src[...]


def body(nx, ny, nz, inputs, proj_weight, out_weight, cotangent, block_history, event_mask):
    half, D = inputs.shape
    T = 2 * half
    CW = D // nx
    RY = D // ny
    RZ = RY // nz
    nblk = half // BLK
    vmem = pl.BlockSpec(memory_space=pltpu.VMEM)
    hbm = pl.BlockSpec(memory_space=pltpu.HBM)
    V = pltpu.VMEM

    def ring_bufs(rows, cols):
        return (
            V((3, rows, cols), BF16),
            V((rows, cols), BF16),
            V((2, rows // 2, cols), F32),
            V((2, rows, cols), BF16),
            V((rows, cols), F32),
        )

    def pair_bufs():
        return V((T, T + TILE), BF16), V((T, T), BF16)

    out_shape = (
        jax.ShapeDtypeStruct((half, CW), BF16),
        jax.ShapeDtypeStruct((half, CW), BF16),
        jax.ShapeDtypeStruct((RZ // 2, 8 * DH), F32),
        jax.ShapeDtypeStruct((RZ // 2, 2 * DH), F32),
    )
    results = pl.pallas_call(
        functools.partial(layer_kernel, nx, ny, nz, half * 2 * ny * nz),
        out_shape=out_shape,
        in_specs=[hbm] * 4 + [pl.BlockSpec(memory_space=pltpu.SMEM), vmem],
        out_specs=(vmem,) * 4,
        scratch_shapes=[
            V((D, 2 * DH), BF16),
            V((D, 8 * DH), BF16),
            V((T, D), BF16),
            V((T, D), BF16),
            V((D, T), BF16),
            V((DH, T), BF16),
            V((2, 8, BLK), jnp.int32),
            V((5, 8, BLK), jnp.int32),
            V((5, 8, T), F32),
            V((T, DH), F32),
            V((T, 4 * DH), F32),
            V((T, DH), BF16),
            V((3, T, 2 * DH), BF16),
            V((3, T, DH), BF16),
            V((3, T, DH), BF16),
            V((T, DH), F32),
            V((T, DH), F32),
            V((2, 2 * nx, 8, half // 2), F32),
            V((T, DH), BF16),
            V((half, 2 * DH), BF16),
            V((T, 4 * DH), BF16),
            V((half, 8 * DH), BF16),
            V((T, DH), F32),
            V((T, DH), F32),
            V((T, DH), F32),
            ring_bufs(half, CW),
            ring_bufs(half, CW),
            ring_bufs(RY, 5 * DH),
            V((RY, 5 * DH), BF16),
            V((2, nz, RZ // 2, 5 * DH), BF16),
            pair_bufs(),
            pair_bufs(),
            pair_bufs(),
            pltpu.SemaphoreType.DMA((11,)),
            pltpu.SemaphoreType.DMA((MAX_COPIES,)),
            pltpu.SemaphoreType.DMA((MAX_COPIES,)),
        ],
        compiler_params=pltpu.CompilerParams(
            collective_id=0, has_side_effects=True, vmem_limit_bytes=60 * 1024 * 1024
        ),
    )(
        inputs,
        proj_weight,
        out_weight,
        cotangent,
        block_history,
        event_mask.reshape(nblk, BLK),
    )
    return pl.pallas_call(
        hand_on,
        out_shape=out_shape,
        in_specs=[vmem] * 4,
        out_specs=(vmem,) * 4,
    )(*results)


def solution(mesh):
    nx = mesh.shape["head"]
    chips = mesh.shape["seq"] // 2
    nz = 8 if chips % 32 == 0 else 2
    ny = chips // nz
    return jax.shard_map(
        functools.partial(body, nx, ny, nz),
        mesh=mesh,
        in_specs=(
            P("seq", None),
            P(None, "head"),
            P(None, "head"),
            P("seq", None),
            P("seq"),
            P("seq"),
        ),
        out_specs=(P("seq", "head"), P("seq", "head"), P("seq", "head"), P("seq", "head")),
        check_vma=False,
    )
```
